32 devices in a mesh: dp: 4 (over z), ctx: 8 (over y, x, core).
Axes of the slice: x: 2, y: 2, z: 4, core: 2. Of those that a mesh axis runs over, the one named last changes fastest.
Arguments:
- q_proj: bfloat16 [4, 1024, 4096], P('dp', 'ctx'), may hold values from -6 to 6
- k_proj: bfloat16 [4, 1024, 4096], P('dp', 'ctx'), may hold values from -6 to 6
- v_proj: bfloat16 [4, 1024, 4096], P('dp', 'ctx'), may hold values from -6 to 6
- out_grad: bfloat16 [4, 1024, 4096], P('dp', 'ctx'), may hold values from -6 to 6
- residue: float32 [16, 4096], replicated, may hold values from -1.5 to 1.5
- pole_decay: float32 [16, 4096], replicated, may hold values from 0.00390625 to 1024
- group_doc: int32 [4, 8], P('dp'), may hold values from 0 to 1, never falling along the last dimension, each value on 1 to 5 neighbouring positions
Outputs:
- mixed: bfloat16 [4, 1024, 4096], P('dp', 'ctx')
- q_grad: bfloat16 [4, 1024, 4096], P('dp', 'ctx')
- k_grad: bfloat16 [4, 1024, 4096], P('dp', 'ctx')
- v_grad: bfloat16 [4, 1024, 4096], P('dp', 'ctx')
- residue_grad: float32 [16, 4096], replicated
- pole_grad: float32 [16, 4096], replicated
The draws below stay inside these ranges and needn't reach their ends.
Inputs may be any that keep to these rules, and one draw needn't show every extreme that they name: group_doc[r, j] numbers the packed sequence that holds block j of row r (tokens j * 128 to (j + 1) * 128 - 1); it never falls along a row, every number appears, each sequence covers 1 to 5 consecutive blocks.
All inputs are finite; a program needn't handle non-finite values.
Results may differ from the reference program's by a relative error of at most 0.001.
Values sent between devices are 32-bit elements; how exact they have to be, the bound alone decides.
No kernel may reach another device: no remote copies, remote signals or barrier semaphores. Data moves between devices by JAX's collectives and lax.ppermute only.
A program may use at most 128 MiB of HBM per device.

```python
import math
import jax
import jax.numpy as jnp
import numpy as np
from jax import lax

C = 4096
M = 16
TOK_DEV = 128
ROW = 1024
TOKENS = 4096
DOCS = 2
MOST_GROUPS = 5
N_DP = 4
N_CTX = 8


def draw_pole_decay(key, part):
    key = jax.random.fold_in(key, 7)
    key_levels, key_first, key_second = jax.random.split(key, 3)
    levels = jax.random.uniform(key_levels, (M, C), jnp.float32)
    first_mode = jax.random.randint(key_first, (C,), 0, M)
    second_mode = (first_mode + jax.random.randint(key_second, (C,), 1, M)) % M
    mode_rows = jnp.arange(M)[:, None]
    levels = jnp.where(mode_rows == first_mode[None, :], 0.0, jnp.where(mode_rows == second_mode[None, :], 1.0, levels))
    lowest = 0.00390625
    highest = float(ROW)
    values = lowest * jnp.exp(levels * math.log(highest / lowest))
    return jnp.clip(values, lowest, highest).astype(jnp.float32)


def block_scale(rng, dims, shards, low, largest):
    def one(dim, shards_of):
        draws = jax.random.uniform(jax.random.fold_in(jax.random.fold_in(rng, 6), dim), (shards_of,), jnp.float32, low / len(shards), largest / len(shards))
        return jnp.repeat(jnp.exp(draws), dims[dim] // shards_of).reshape((-1,) + (1,) * (len(dims) - dim - 1))

    loudness = one(*shards[0])
    for cut in shards[1:]:
        loudness = loudness * one(*cut)
    return loudness


def split_up(amount, total, reach, skew):
    loads = [(1 << 20) // math.isqrt(standing ** skew) + 1 for standing in range(2, amount + 1)]
    surplus, holding = total - reach - (amount - 1), [1] * (amount - 1)
    while surplus > 0:
        candidates = [i for i in range(amount - 1) if holding[i] < reach]
        pool, budget = sum([loads[i] for i in candidates]), surplus
        for i in candidates:
            more = min(reach - holding[i], max(1, budget * loads[i] // pool), surplus)
            holding[i] = holding[i] + more
            surplus = surplus - more
    return np.array([reach] + holding)


def uneven(rng, count, total, bound, lean):
    if count == 2:
        one = jax.random.randint(rng, (), max(1, total - bound), min(bound, total - 1) + 1)
        return jnp.stack([one, total - one])
    lengths = jnp.asarray(split_up(count, total, bound, lean), jnp.int32)
    twos = (count - 1) // 2
    giver, taker = lengths[1:1 + 2 * twos:2], lengths[2:2 + 2 * twos:2]
    room = jnp.minimum(giver - 1, bound - taker)
    moved = jax.random.randint(jax.random.fold_in(rng, 1), (twos,), 0, 1 << 20) % (room + 1)
    lengths = lengths.at[1:1 + 2 * twos:2].set(giver - moved).at[2:2 + 2 * twos:2].set(taker + moved)
    return lengths[jax.random.permutation(jax.random.fold_in(rng, 2), count)]


def noise(own_key, dims, spread, reach, cuts=(), kind=jnp.bfloat16):
    drawn = jax.random.normal(own_key, dims, jnp.float32) * spread
    if len(cuts) > 0:
        drawn = block_scale(own_key, dims, cuts, -0.22, 0.18) * drawn
    return jnp.clip(drawn, min=-reach, max=reach).astype(kind)


def setup_inputs(seed: int = 0) -> dict:
    streams_of = jax.random.split(jax.random.key(seed), 8)
    return {
        "q_proj": noise(streams_of[0], (N_DP, ROW, C), 1.0, 6.0, ((0, 4), (1, 8))),
        "k_proj": noise(streams_of[1], (N_DP, ROW, C), 1.0, 6.0, ((0, 4), (1, 8))),
        "v_proj": noise(streams_of[2], (N_DP, ROW, C), 1.0, 6.0, ((0, 4), (1, 8))),
        "out_grad": noise(streams_of[3], (N_DP, ROW, C), 1.0, 6.0, ((0, 4), (1, 8))),
        "residue": noise(streams_of[4], (M, C), M ** -0.5, 1.5, (), jnp.float32),
        "pole_decay": draw_pole_decay(jax.random.fold_in(streams_of[7], 71), 0),
        "group_doc": jax.vmap(lambda own: jnp.searchsorted(jnp.cumsum(uneven(own, DOCS, N_CTX, MOST_GROUPS, 2)), jnp.arange(N_CTX), side="right"))(jax.random.split(streams_of[6], N_DP)).reshape((N_DP, N_CTX)).astype(jnp.int32),
    }


def reference(q_proj, k_proj, v_proj, out_grad, residue, pole_decay, group_doc):
    decay_rate = pole_decay / ROW
    factor = jnp.exp(-decay_rate)
    residue_eff = residue * jnp.sqrt(2.0 * decay_rate)
    query = q_proj.astype(jnp.float32)
    key_in = k_proj.astype(jnp.float32)
    value_in = v_proj.astype(jnp.float32)
    cotangent = out_grad.astype(jnp.float32)
    mixed_in = key_in * value_in
    gate_grad = cotangent * query
    doc_of = jnp.repeat(group_doc, TOK_DEV, axis=1)
    joined = (doc_of[:, 1:] == doc_of[:, :-1]).astype(jnp.float32)
    first_col = jnp.zeros((N_DP, 1), jnp.float32)
    cont_prev = jnp.concatenate([first_col, joined], axis=1)
    cont_next = jnp.concatenate([joined, first_col], axis=1)
    mixed_time = jnp.swapaxes(mixed_in, 0, 1)
    grad_time = jnp.swapaxes(gate_grad, 0, 1)

    def forward_step(carried, inputs):
        state, state_lag, grad_res, grad_lag = carried
        mix_now, grad_now, keep_now = inputs
        keep = keep_now[:, None, None]
        state_lag = keep * factor * (state_lag + state)
        state = keep * factor * state + mix_now[:, None, :]
        grad_res = grad_res + grad_now[:, None, :] * state
        grad_lag = grad_lag + grad_now[:, None, :] * state_lag
        conv_now = lax.optimization_barrier(jnp.sum(residue_eff * state, axis=1))
        return ((state, state_lag, grad_res, grad_lag), conv_now)
    empty = jnp.zeros((N_DP, M, C), jnp.float32)
    carried, conv_time = lax.scan(forward_step, (empty, empty, empty, empty), (mixed_time, grad_time, cont_prev.T))
    grad_res = lax.optimization_barrier(jnp.sum(carried[2], axis=0))
    grad_lag = lax.optimization_barrier(jnp.sum(carried[3], axis=0))

    def backward_step(back_state, inputs):
        grad_now, keep_now = inputs
        back_state = keep_now[:, None, None] * factor * back_state + grad_now[:, None, :]
        return (back_state, lax.optimization_barrier(jnp.sum(residue_eff * back_state, axis=1)))
    _, back_time = lax.scan(backward_step, empty, (grad_time, cont_next.T), reverse=True)
    conv = jnp.swapaxes(conv_time, 0, 1)
    conv_grad = jnp.swapaxes(back_time, 0, 1)
    mixed = (query * conv).astype(jnp.bfloat16)
    q_grad = (cotangent * conv).astype(jnp.bfloat16)
    k_grad = (conv_grad * value_in).astype(jnp.bfloat16)
    v_grad = (conv_grad * key_in).astype(jnp.bfloat16)
    scale = 1.0 / math.sqrt(TOKENS)
    residue_grad = jnp.sqrt(2.0 * decay_rate) * grad_res * scale
    pole_grad = residue_eff * (0.5 * grad_res - decay_rate * grad_lag) * scale
    return (mixed, q_grad, k_grad, v_grad, residue_grad, pole_grad)
```

```python
from functools import partial
import math

import jax
import jax.numpy as jnp
from jax import lax
from jax.experimental import pallas as pl
from jax.experimental.pallas import tpu as pltpu
from jax.sharding import PartitionSpec as P

F32 = jnp.float32
LANES = 128
SUBS = 8
GROUP = LANES * SUBS
CHUNK = 8
VMEM_BYTES = 48 * 1024 * 1024


def to_rows(left_ref, right_ref, rows_ref):
    tokens = left_ref.shape[0]
    for pair in range(tokens // 16):
        window = pl.ds(pair * 16, 16)
        for tile in range(SUBS):
            lanes = pl.ds(tile * LANES, LANES)
            product = left_ref[window, lanes].astype(F32) * right_ref[window, lanes].astype(F32)
            for part in range(2):
                start = (pair * 2 + part) * 64 + tile * 8
                rows_ref[pl.ds(start, 8), :] = product[part * 8 : part * 8 + 8]


def token_row(rows_ref, chunk, token):
    return rows_ref[pl.ds(chunk * 64 + token, 8, stride=8), :]


def stats_kernel(
    row_len, k_ref, v_ref, q_ref, g_ref, pole_ref, c_ref, b_ref, st_ref,
    u_rows, d_rows, lam_s, jump_s, slope_s, state_s, lag_s, res_s, mixl_s, head_s, headl_s, headm_s, pow_s, corr_s,
):
    modes = pole_ref.shape[0]
    chunks = k_ref.shape[0] // CHUNK
    to_rows(k_ref, v_ref, u_rows)
    to_rows(g_ref, q_ref, d_rows)
    zero = jnp.zeros((SUBS, LANES), F32)
    for m in range(modes):
        rate = pole_ref[m] / row_len
        lam_s[m] = jnp.exp(-rate)
        jump_s[m] = jnp.exp(-CHUNK * rate)
        slope_s[m] = CHUNK * jnp.exp(-(CHUNK - 1) * rate)
        for ref in (state_s, lag_s, res_s, mixl_s, head_s, headl_s, headm_s):
            ref[m] = zero
        pow_s[m] = zero + 1.0
    for lag in range(CHUNK):
        corr_s[lag] = zero

    def step(chunk, _):
        u = [token_row(u_rows, chunk, t) for t in range(CHUNK)]
        d = [token_row(d_rows, chunk, t) for t in range(CHUNK)]
        for lag in range(CHUNK):
            total = corr_s[lag]
            for t in range(CHUNK - lag):
                total = total + d[t + lag] * u[t]
            corr_s[lag] = total
        offset = (chunk * CHUNK).astype(F32)
        for m in range(modes):
            lam = lam_s[m]
            end, endl = u[0], None
            for t in range(1, CHUNK):
                endl = end if endl is None else endl * lam + end
                end = end * lam + u[t]
            head, headl = d[CHUNK - 1], None
            for t in range(CHUNK - 2, -1, -1):
                headl = head if headl is None else headl * lam + head
                head = head * lam + d[t]
            c_ref[chunk, m] = end
            b_ref[chunk, m] = head
            state, lag_state = state_s[m], lag_s[m]
            res_s[m] = res_s[m] + head * state
            mixl_s[m] = mixl_s[m] + (headl * state + head * lag_state)
            jump = jump_s[m]
            lag_s[m] = lag_state * jump + (state * slope_s[m] + endl)
            state_s[m] = state * jump + end
            power = pow_s[m]
            far = power * head
            head_s[m] = head_s[m] + far
            headl_s[m] = headl_s[m] + power * headl
            headm_s[m] = headm_s[m] + offset * far
            pow_s[m] = power * jump
        return 0

    lax.fori_loop(0, chunks, step, 0)
    for m in range(modes):
        lam = lam_s[m]
        st_ref[0, m] = state_s[m]
        st_ref[1, m] = lam * lag_s[m]
        st_ref[2, m] = head_s[m]
        st_ref[3, m] = lam * headl_s[m] + headm_s[m]
        near, nearl = corr_s[CHUNK - 1], None
        for lag in range(CHUNK - 2, -1, -1):
            nearl = near if nearl is None else nearl * lam + near
            near = near * lam + corr_s[lag]
        res = res_s[m]
        st_ref[4, m] = near + lam * res
        st_ref[5, m] = lam * (nearl + (res + lam * mixl_s[m]))


def output_kernel(
    row_len, core_ref, k_ref, v_ref, q_ref, g_ref, pole_ref, residue_ref, c_ref, b_ref, kept_ref, got_ref,
    mixed_ref, qg_ref, kg_ref, vg_ref,
    u_rows, d_rows, z_rows, w_rows, lam_s, jump_s, lead_s, state_s, back_s, tap_s,
):
    modes = pole_ref.shape[0]
    half = modes // 2
    chunks = k_ref.shape[0] // CHUNK
    first = core_ref[0] == 0
    to_rows(k_ref, v_ref, u_rows)
    to_rows(g_ref, q_ref, d_rows)
    taps = [jnp.zeros((SUBS, LANES), F32) for _ in range(CHUNK)]
    for m in range(modes):
        rate = pole_ref[m] / row_len
        lam = jnp.exp(-rate)
        lam_s[m] = lam
        jump_s[m] = jnp.exp(-CHUNK * rate)
        power = residue_ref[m] * jnp.sqrt(2.0 * rate)
        lead_s[m] = power * lam
        for lag in range(CHUNK):
            taps[lag] = taps[lag] + power
            power = power * lam
        mine = first if m < half else jnp.logical_not(first)
        state_s[m] = jnp.where(mine, kept_ref[0, m % half], got_ref[0, m % half])
        back_s[m] = jnp.where(mine, kept_ref[1, m % half], got_ref[1, m % half])
    for lag in range(CHUNK):
        tap_s[lag] = taps[lag]

    def ahead(chunk, _):
        u = [token_row(u_rows, chunk, t) for t in range(CHUNK)]
        z = [None] * CHUNK
        for lag in range(CHUNK):
            tap = tap_s[lag]
            for t in range(lag, CHUNK):
                term = tap * u[t - lag]
                z[t] = term if z[t] is None else z[t] + term
        for m in range(modes):
            lam = lam_s[m]
            state = state_s[m]
            term = state * lead_s[m]
            for t in range(CHUNK):
                z[t] = z[t] + term
                if t + 1 < CHUNK:
                    term = term * lam
            state_s[m] = state * jump_s[m] + c_ref[chunk, m]
        for t in range(CHUNK):
            z_rows[pl.ds(chunk * 64 + t, 8, stride=8), :] = z[t]
        return 0

    def behind(index, _):
        chunk = chunks - 1 - index
        d = [token_row(d_rows, chunk, t) for t in range(CHUNK)]
        w = [None] * CHUNK
        for lag in range(CHUNK):
            tap = tap_s[lag]
            for t in range(CHUNK - lag):
                term = tap * d[t + lag]
                w[t] = term if w[t] is None else w[t] + term
        for m in range(modes):
            lam = lam_s[m]
            back = back_s[m]
            term = back * lead_s[m]
            for t in range(CHUNK - 1, -1, -1):
                w[t] = w[t] + term
                if t > 0:
                    term = term * lam
            back_s[m] = back * jump_s[m] + b_ref[chunk, m]
        for t in range(CHUNK):
            w_rows[pl.ds(chunk * 64 + t, 8, stride=8), :] = w[t]
        return 0

    lax.fori_loop(0, chunks, ahead, 0)
    lax.fori_loop(0, chunks, behind, 0)
    for pair in range(chunks // 2):
        window = pl.ds(pair * 16, 16)
        for tile in range(SUBS):
            lanes = pl.ds(tile * LANES, LANES)
            z = jnp.concatenate([z_rows[pl.ds((pair * 2 + part) * 64 + tile * 8, 8), :] for part in range(2)], axis=0)
            w = jnp.concatenate([w_rows[pl.ds((pair * 2 + part) * 64 + tile * 8, 8), :] for part in range(2)], axis=0)
            mixed_ref[window, lanes] = (q_ref[window, lanes].astype(F32) * z).astype(jnp.bfloat16)
            qg_ref[window, lanes] = (g_ref[window, lanes].astype(F32) * z).astype(jnp.bfloat16)
            kg_ref[window, lanes] = (w * v_ref[window, lanes].astype(F32)).astype(jnp.bfloat16)
            vg_ref[window, lanes] = (w * k_ref[window, lanes].astype(F32)).astype(jnp.bfloat16)


def merge_kernel(row_len, block, info_ref, kept_ref, got_ref, pole_ref, chip_ref):
    first = info_ref[0] == 0
    joined = (info_ref[2] == info_ref[3]).astype(F32)
    rate = pole_ref[...] / row_len
    lam = jnp.exp(-rate)
    hop = joined * jnp.exp(-block * rate)
    link = joined * lam
    left = [jnp.where(first, kept_ref[i], got_ref[i]) for i in range(6)]
    right = [jnp.where(first, got_ref[i], kept_ref[i]) for i in range(6)]
    chip_ref[0] = right[0] + hop * left[0]
    chip_ref[1] = right[1] + hop * (left[1] + block * left[0])
    chip_ref[2] = left[2] + hop * right[2]
    chip_ref[3] = left[3] + hop * (right[3] + block * right[2])
    chip_ref[4] = left[4] + right[4] + link * (right[2] * left[0])
    chip_ref[5] = left[5] + right[5] + link * ((right[3] + right[2]) * left[0] + right[2] * left[1])


def scan_kernel(row_len, block, chips, info_ref, doc_ref, pole_ref, *refs):
    ins, outs, total_ref = refs[:chips], refs[chips : 2 * chips], refs[2 * chips]
    ordered, ends = refs[2 * chips + 1], refs[2 * chips + 2]
    chip = info_ref[1]
    for away in range(chips):
        ordered[chip ^ away] = ins[away][...]
    rate = pole_ref[...] / row_len
    lam = jnp.exp(-rate)
    span = 2.0 * block
    hop = jnp.exp(-span * rate)
    zero = jnp.zeros_like(rate)
    state, lag_state, res, grad_lag = zero, zero, zero, zero
    for j in range(chips):
        ends[j, 0] = state
        res = res + (ordered[j, 4] + lam * (ordered[j, 2] * state))
        grad_lag = grad_lag + (
            ordered[j, 5]
            + lam * ((ordered[j, 3] + ordered[j, 2]) * state + ordered[j, 2] * lag_state)
        )
        if j + 1 < chips:
            through = (doc_ref[0, 2 * j] == doc_ref[0, 2 * j + 1]).astype(F32) * hop
            keep = (doc_ref[0, 2 * j + 1] == doc_ref[0, 2 * j + 2]).astype(F32)
            lag_state = keep * (ordered[j, 1] + through * (lag_state + span * state))
            state = keep * (ordered[j, 0] + through * state)
    back = zero
    for j in range(chips - 1, -1, -1):
        ends[j, 1] = back
        if j > 0:
            through = (doc_ref[0, 2 * j] == doc_ref[0, 2 * j + 1]).astype(F32) * hop
            keep = (doc_ref[0, 2 * j - 1] == doc_ref[0, 2 * j]).astype(F32)
            back = keep * (ordered[j, 2] + through * back)
    for away in range(chips):
        outs[away][...] = ends[chip ^ away]
    total_ref[0] = res
    total_ref[1] = grad_lag


def expand_kernel(row_len, block, chips, info_ref, pole_ref, kept_ref, got_ref, *refs):
    ins, mine_ref, send_ref, whole = refs[:chips], refs[chips], refs[chips + 1], refs[chips + 2]
    first = info_ref[0] == 0
    chip = info_ref[1]
    joined = (info_ref[2] == info_ref[3]).astype(F32)
    part = ins[0].shape[1]
    for away in range(chips):
        start = pl.multiple_of((chip ^ away) * part, part)
        whole[:, pl.ds(start, part), :] = ins[away][...]
    hop = joined * jnp.exp(-block * (pole_ref[...] / row_len))
    end_left = jnp.where(first, kept_ref[0], got_ref[0])
    head_right = jnp.where(first, got_ref[2], kept_ref[2])
    state, back = whole[0], whole[1]
    state_right = joined * end_left + hop * state
    back_left = joined * head_right + hop * back
    mine_ref[0] = jnp.where(first, state, state_right)
    mine_ref[1] = jnp.where(first, back_left, back)
    send_ref[0] = jnp.where(first, state_right, state)
    send_ref[1] = jnp.where(first, back, back_left)


def gather_kernel(chips, info_ref, *refs):
    ins, out_ref = refs[:chips], refs[chips]
    chip = info_ref[1]
    part = ins[0].shape[1]
    for away in range(chips):
        start = pl.multiple_of((chip ^ away) * part, part)
        out_ref[:, pl.ds(start, part), :] = ins[away][...]


def final_kernel(row_len, scale, info_ref, pole_ref, residue_ref, kept_ref, got_ref, res_ref, grad_ref):
    first = info_ref[0] == 0
    half = kept_ref.shape[1]
    for part in range(2):
        mine = first if part == 0 else jnp.logical_not(first)
        rows = pl.ds(part * half, half)
        grad_res = jnp.where(mine, kept_ref[0], got_ref[0])
        grad_lag = jnp.where(mine, kept_ref[1], got_ref[1])
        rate = pole_ref[rows, :] / row_len
        root = jnp.sqrt(2.0 * rate)
        res_ref[rows, :] = root * grad_res * scale
        grad_ref[rows, :] = residue_ref[rows, :] * root * (0.5 * grad_res - rate * grad_lag) * scale


def whole_spec():
    return pl.BlockSpec(memory_space=pltpu.VMEM)


def scalar_spec():
    return pl.BlockSpec(memory_space=pltpu.SMEM)


def params():
    return pltpu.CompilerParams(vmem_limit_bytes=VMEM_BYTES)


def body(q_proj, k_proj, v_proj, out_grad, residue, pole_decay, group_doc):
    block, channels = q_proj.shape[1], q_proj.shape[2]
    modes = residue.shape[0]
    n_ctx, n_dp = lax.axis_size("ctx"), lax.axis_size("dp")
    row_len = block * n_ctx
    total_tokens = row_len * n_dp
    chips = n_ctx // 2
    groups = channels // GROUP
    chunks = block // CHUNK
    tall = channels // LANES
    rows = modes * tall
    half = rows // 2
    part = half // chips

    me = lax.axis_index("ctx").astype(jnp.int32)
    core, chip = me % 2, me // 2
    docs = lax.dynamic_slice(group_doc, (0, chip * 2), (1, 2))
    info = jnp.stack([core, chip, docs[0, 0], docs[0, 1]]).astype(jnp.int32)
    pole = pole_decay.reshape(modes, tall, LANES)
    resid = residue.reshape(modes, tall, LANES)
    pole_rows, resid_rows = pole.reshape(rows, LANES), resid.reshape(rows, LANES)

    k_in, v_in, q_in, g_in = (x.reshape(block, channels) for x in (k_proj, v_proj, q_proj, out_grad))
    wide = pl.BlockSpec((block, GROUP), lambda i: (0, i))
    slim = pl.BlockSpec((modes, SUBS, LANES), lambda i: (0, i, 0))
    chunked = pl.BlockSpec((chunks, modes, SUBS, LANES), lambda i: (0, 0, i, 0))
    row_scratch = pltpu.VMEM((block * SUBS, LANES), F32)
    mode_scratch = pltpu.VMEM((modes, SUBS, LANES), F32)
    tap_scratch = pltpu.VMEM((CHUNK, SUBS, LANES), F32)

    ends, heads, stats = pl.pallas_call(
        partial(stats_kernel, float(row_len)),
        grid=(groups,),
        in_specs=[wide] * 4 + [slim],
        out_specs=[chunked, chunked, pl.BlockSpec((6, modes, SUBS, LANES), lambda i: (0, 0, i, 0))],
        out_shape=[
            jax.ShapeDtypeStruct((chunks, modes, tall, LANES), F32),
            jax.ShapeDtypeStruct((chunks, modes, tall, LANES), F32),
            jax.ShapeDtypeStruct((6, modes, tall, LANES), F32),
        ],
        scratch_shapes=[row_scratch] * 2 + [mode_scratch] * 11 + [tap_scratch],
        compiler_params=params(),
        name="block_stats",
    )(k_in, v_in, q_in, g_in, pole)

    stats = stats.reshape(6, rows, LANES)

    def swap_core(x):
        return lax.ppermute(x, "ctx", [(i, i ^ 1) for i in range(n_ctx)])

    def swap_chip(x, away):
        return lax.ppermute(x, "ctx", [(i, i ^ (2 * away)) for i in range(n_ctx)])

    kept = lax.dynamic_slice(stats, (0, core * half, 0), (6, half, LANES))
    got = swap_core(lax.dynamic_slice(stats, (0, (1 - core) * half, 0), (6, half, LANES)))
    pole_half = lax.dynamic_slice(pole_rows, (core * half, 0), (half, LANES))
    merged = pl.pallas_call(
        partial(merge_kernel, float(row_len), float(block)),
        in_specs=[scalar_spec()] + [whole_spec()] * 3,
        out_specs=whole_spec(),
        out_shape=jax.ShapeDtypeStruct((6, half, LANES), F32),
        compiler_params=params(),
        name="chip_stats",
    )(info, kept, got, pole_half)

    def cut(away):
        return lax.dynamic_slice(merged, (0, (chip ^ away) * part, 0), (6, part, LANES))

    pieces = [cut(0)] + [swap_chip(cut(away), away) for away in range(1, chips)]
    pole_part = lax.dynamic_slice(pole_half, (chip * part, 0), (part, LANES))
    scanned = pl.pallas_call(
        partial(scan_kernel, float(row_len), float(block), chips),
        in_specs=[scalar_spec(), scalar_spec()] + [whole_spec()] * (1 + chips),
        out_specs=[whole_spec()] * (chips + 1),
        out_shape=[jax.ShapeDtypeStruct((2, part, LANES), F32)] * (chips + 1),
        scratch_shapes=[pltpu.VMEM((chips, 6, part, LANES), F32), pltpu.VMEM((chips, 2, part, LANES), F32)],
        compiler_params=params(),
        name="row_scan",
    )(info, group_doc, pole_part, *pieces)

    edges = [scanned[0]] + [swap_chip(scanned[away], away) for away in range(1, chips)]
    mine, send = pl.pallas_call(
        partial(expand_kernel, float(row_len), float(block), chips),
        in_specs=[scalar_spec()] + [whole_spec()] * (3 + chips),
        out_specs=[whole_spec()] * 2,
        out_shape=[jax.ShapeDtypeStruct((2, half, LANES), F32)] * 2,
        scratch_shapes=[pltpu.VMEM((2, half, LANES), F32)],
        compiler_params=params(),
        name="block_edges",
    )(info, pole_half, kept, got, *edges)
    theirs = swap_core(send)

    total = scanned[chips]
    reach = 1
    while reach < n_dp:
        total = total + lax.ppermute(total, "dp", [(i, i ^ reach) for i in range(n_dp)])
        reach *= 2
    sums = [total] + [swap_chip(total, away) for away in range(1, chips)]
    gathered = pl.pallas_call(
        partial(gather_kernel, chips),
        in_specs=[scalar_spec()] + [whole_spec()] * chips,
        out_specs=whole_spec(),
        out_shape=jax.ShapeDtypeStruct((2, half, LANES), F32),
        compiler_params=params(),
        name="gather_sums",
    )(info, *sums)
    other = swap_core(gathered)

    halves = modes // 2
    edge_spec = pl.BlockSpec((2, halves, SUBS, LANES), lambda i: (0, 0, i, 0))
    outs = pl.pallas_call(
        partial(output_kernel, float(row_len)),
        grid=(groups,),
        in_specs=[scalar_spec()] + [wide] * 4 + [slim] * 2 + [chunked] * 2 + [edge_spec] * 2,
        out_specs=[wide] * 4,
        out_shape=[jax.ShapeDtypeStruct((block, channels), jnp.bfloat16)] * 4,
        scratch_shapes=[row_scratch] * 4 + [mode_scratch] * 5 + [tap_scratch],
        compiler_params=params(),
        cost_estimate=pl.CostEstimate(flops=60_000_000_000, bytes_accessed=20_000_000, transcendentals=0),
        name="outputs",
    )(
        info, k_in, v_in, q_in, g_in, pole, resid, ends, heads,
        mine.reshape(2, halves, tall, LANES), theirs.reshape(2, halves, tall, LANES),
    )

    residue_grad, pole_grad = pl.pallas_call(
        partial(final_kernel, float(row_len), 1.0 / math.sqrt(total_tokens)),
        in_specs=[scalar_spec()] + [whole_spec()] * 4,
        out_specs=[whole_spec()] * 2,
        out_shape=[jax.ShapeDtypeStruct((rows, LANES), F32)] * 2,
        compiler_params=params(),
        name="parameter_grads",
    )(info, pole_rows, resid_rows, gathered, other)
    return (
        *(x[None] for x in outs),
        residue_grad.reshape(modes, channels),
        pole_grad.reshape(modes, channels),
    )


def solution(mesh):
    tokens = P("dp", "ctx", None)
    return jax.shard_map(
        body,
        mesh=mesh,
        in_specs=(tokens, tokens, tokens, tokens, P(), P(), P("dp", None)),
        out_specs=(tokens, tokens, tokens, tokens, P(), P()),
        check_vma=False,
    )
```

```python
from functools import partial
import math

import jax
import jax.numpy as jnp
from jax import lax
from jax.experimental import pallas as pl
from jax.experimental.pallas import tpu as pltpu
from jax.sharding import PartitionSpec as P

F32 = jnp.float32
LANES = 128
SUBS = 8
GROUP = LANES * SUBS
CHUNK = 8
BIG = 60


def to_rows(left_ref, right_ref, rows_ref):
    tokens = left_ref.shape[0]
    for pair in range(tokens // 16):
        window = pl.ds(pair * 16, 16)
        for tile in range(SUBS):
            lanes = pl.ds(tile * LANES, LANES)
            product = left_ref[window, lanes].astype(F32) * right_ref[window, lanes].astype(F32)
            for part in range(2):
                start = (pair * 2 + part) * 64 + tile * 8
                rows_ref[pl.ds(start, 8), :] = product[part * 8 : part * 8 + 8]


def token_row(rows_ref, chunk, token):
    return rows_ref[pl.ds(chunk * 64 + token, 8, stride=8), :]


def mode_rows(natural_ref, rows_ref):
    for eight in range(natural_ref.shape[0] // 8):
        for tile in range(SUBS):
            rows_ref[pl.ds(eight * 64 + tile * 8, 8), :] = natural_ref[
                pl.ds(eight * 8, 8), pl.ds(tile * LANES, LANES)
            ]


def mode_row(rows_ref, mode):
    return rows_ref[pl.ds((mode // 8) * 64 + mode % 8, 8, stride=8), :]


def stats_kernel(
    row_len, k_ref, v_ref, q_ref, g_ref, pole_ref, c_ref, b_ref, rate_ref, kept_ref, send_ref,
    u_rows, d_rows, p_rows, lam_s, jump_s, slope_s, state_s, lag_s, res_s, mixl_s, head_s, headl_s, headm_s, pow_s,
    corr_s,
):
    modes = pole_ref.shape[0]
    chunks = k_ref.shape[0] // CHUNK
    first = lax.axis_index("ctx") % 2 == 0
    to_rows(k_ref, v_ref, u_rows)
    to_rows(g_ref, q_ref, d_rows)
    mode_rows(pole_ref, p_rows)
    zero = jnp.zeros((SUBS, LANES), F32)
    for m in range(modes):
        rate = mode_row(p_rows, m) / row_len
        rate_ref[m] = rate
        lam = jnp.exp(-rate)
        square = lam * lam
        fourth = square * square
        lam_s[m] = lam
        jump_s[m] = fourth * fourth
        slope_s[m] = CHUNK * (fourth * (square * lam))
        for ref in (state_s, lag_s, res_s, mixl_s, head_s, headl_s, headm_s):
            ref[m] = zero
        pow_s[m] = zero + 1.0
    for lag in range(CHUNK):
        corr_s[lag] = zero

    def step(chunk, _):
        u = [token_row(u_rows, chunk, t) for t in range(CHUNK)]
        d = [token_row(d_rows, chunk, t) for t in range(CHUNK)]
        for lag in range(CHUNK):
            total = corr_s[lag]
            for t in range(CHUNK - lag):
                total = total + d[t + lag] * u[t]
            corr_s[lag] = total
        offset = (chunk * CHUNK).astype(F32)
        for m in range(modes):
            lam = lam_s[m]
            end, endl = u[0], None
            for t in range(1, CHUNK):
                endl = end if endl is None else endl * lam + end
                end = end * lam + u[t]
            head, headl = d[CHUNK - 1], None
            for t in range(CHUNK - 2, -1, -1):
                headl = head if headl is None else headl * lam + head
                head = head * lam + d[t]
            c_ref[chunk, m] = end
            b_ref[chunk, m] = head
            state, lag_state = state_s[m], lag_s[m]
            res_s[m] = res_s[m] + head * state
            mixl_s[m] = mixl_s[m] + (headl * state + head * lag_state)
            jump = jump_s[m]
            lag_s[m] = lag_state * jump + (state * slope_s[m] + endl)
            state_s[m] = state * jump + end
            power = pow_s[m]
            far = power * head
            head_s[m] = head_s[m] + far
            headl_s[m] = headl_s[m] + power * headl
            headm_s[m] = headm_s[m] + offset * far
            pow_s[m] = power * jump
        return 0

    lax.fori_loop(0, chunks, step, 0)
    def stats_of(m):
        lam = lam_s[m]
        near, nearl = corr_s[CHUNK - 1], None
        for lag in range(CHUNK - 2, -1, -1):
            nearl = near if nearl is None else nearl * lam + near
            near = near * lam + corr_s[lag]
        res = res_s[m]
        return (
            state_s[m],
            lam * lag_s[m],
            head_s[m],
            lam * headl_s[m] + headm_s[m],
            near + lam * res,
            lam * (nearl + (res + lam * mixl_s[m])),
        )

    half = modes // 2
    for m in range(half):
        kept_ref[6, m] = jnp.where(first, rate_ref[m], rate_ref[m + half])
        for i, (low, high) in enumerate(zip(stats_of(m), stats_of(m + half))):
            kept_ref[i, m] = jnp.where(first, low, high)
            send_ref[i, m] = jnp.where(first, high, low)


def local_kernel(
    k_ref, v_ref, q_ref, g_ref, rate_ref, residue_ref, c_ref, b_ref, after_ref,
    z_ref, w_ref, zeros_ref, u_rows, d_rows, r_rows, lam_s, jump_s, lead_s, state_s, back_s, tap_s,
):
    modes = rate_ref.shape[0]
    chunks = k_ref.shape[0] // CHUNK
    zeros_ref[...] = jnp.zeros((1, LANES), F32)
    to_rows(k_ref, v_ref, u_rows)
    to_rows(g_ref, q_ref, d_rows)
    mode_rows(residue_ref, r_rows)
    zero = jnp.zeros((SUBS, LANES), F32)
    taps = [zero for _ in range(CHUNK)]
    for m in range(modes):
        rate = rate_ref[m]
        lam = jnp.exp(-rate)
        square = lam * lam
        fourth = square * square
        lam_s[m] = lam
        jump_s[m] = fourth * fourth
        power = mode_row(r_rows, m) * jnp.sqrt(2.0 * rate)
        lead_s[m] = power * lam
        for lag in range(CHUNK):
            taps[lag] = taps[lag] + power
            power = power * lam
        state_s[m] = zero
        back_s[m] = zero
    for lag in range(CHUNK):
        tap_s[lag] = taps[lag]

    def ahead(chunk, _):
        u = [token_row(u_rows, chunk, t) for t in range(CHUNK)]
        z = [None] * CHUNK
        for lag in range(CHUNK):
            tap = tap_s[lag]
            for t in range(lag, CHUNK):
                term = tap * u[t - lag]
                z[t] = term if z[t] is None else z[t] + term
        for m in range(modes):
            lam = lam_s[m]
            state = state_s[m]
            term = state * lead_s[m]
            for t in range(CHUNK):
                z[t] = z[t] + term
                if t + 1 < CHUNK:
                    term = term * lam
            state_s[m] = state * jump_s[m] + c_ref[chunk, m]
        for t in range(CHUNK):
            z_ref[0, chunk * CHUNK + t] = z[t]
        return 0

    def behind(index, _):
        chunk = chunks - 1 - index
        d = [token_row(d_rows, chunk, t) for t in range(CHUNK)]
        w = [None] * CHUNK
        for lag in range(CHUNK):
            tap = tap_s[lag]
            for t in range(CHUNK - lag):
                term = tap * d[t + lag]
                w[t] = term if w[t] is None else w[t] + term
        for m in range(modes):
            lam = lam_s[m]
            back = back_s[m]
            term = back * lead_s[m]
            for t in range(CHUNK - 1, -1, -1):
                w[t] = w[t] + term
                if t > 0:
                    term = term * lam
            back_s[m] = back * jump_s[m] + b_ref[chunk, m]
        for t in range(CHUNK):
            w_ref[0, chunk * CHUNK + t] = w[t]
        return 0

    lax.fori_loop(0, chunks, ahead, 0)
    lax.fori_loop(0, chunks, behind, 0)


def output_kernel(
    earlier, k_ref, v_ref, q_ref, g_ref, rate_ref, residue_ref, zl_ref, wl_ref, kept_ref, got_ref, after_ref, *refs
):
    mixed_ref, qg_ref, kg_ref, vg_ref, zeros_ref = refs[earlier : earlier + 5]
    z_rows, w_rows, r_rows, lam_s, ahead_s, behind_s = refs[earlier + 5 :]
    modes = rate_ref.shape[0]
    half = modes // 2
    chunks = k_ref.shape[0] // CHUNK
    first = lax.axis_index("ctx") % 2 == 0
    zeros_ref[...] = jnp.zeros((1, LANES), F32)
    mode_rows(residue_ref, r_rows)
    for m in range(modes):
        rate = rate_ref[m]
        lam = jnp.exp(-rate)
        lam_s[m] = lam
        lead = mode_row(r_rows, m) * jnp.sqrt(2.0 * rate) * lam
        mine = first if m < half else jnp.logical_not(first)
        ahead_s[m] = lead * jnp.where(mine, kept_ref[0, m % half], got_ref[0, m % half])
        behind_s[m] = lead * jnp.where(mine, kept_ref[1, m % half], got_ref[1, m % half])

    def step(chunk, _):
        mirror = chunks - 1 - chunk
        z = [zl_ref[0, chunk * CHUNK + t] for t in range(CHUNK)]
        w = [wl_ref[0, mirror * CHUNK + t] for t in range(CHUNK)]
        for m in range(modes):
            lam = lam_s[m]
            ahead, behind = ahead_s[m], behind_s[m]
            for t in range(CHUNK):
                z[t] = z[t] + ahead
                ahead = ahead * lam
                w[CHUNK - 1 - t] = w[CHUNK - 1 - t] + behind
                behind = behind * lam
            ahead_s[m] = ahead
            behind_s[m] = behind
        for t in range(CHUNK):
            z_rows[pl.ds(chunk * 64 + t, 8, stride=8), :] = z[t]
            w_rows[pl.ds(mirror * 64 + t, 8, stride=8), :] = w[t]
        return 0

    lax.fori_loop(0, chunks, step, 0)
    for pair in range(chunks // 2):
        window = pl.ds(pair * 16, 16)
        for tile in range(SUBS):
            lanes = pl.ds(tile * LANES, LANES)
            z = jnp.concatenate([z_rows[pl.ds((pair * 2 + part) * 64 + tile * 8, 8), :] for part in range(2)], axis=0)
            w = jnp.concatenate([w_rows[pl.ds((pair * 2 + part) * 64 + tile * 8, 8), :] for part in range(2)], axis=0)
            mixed_ref[window, lanes] = (q_ref[window, lanes].astype(F32) * z).astype(jnp.bfloat16)
            qg_ref[window, lanes] = (g_ref[window, lanes].astype(F32) * z).astype(jnp.bfloat16)
            kg_ref[window, lanes] = (w * v_ref[window, lanes].astype(F32)).astype(jnp.bfloat16)
            vg_ref[window, lanes] = (w * k_ref[window, lanes].astype(F32)).astype(jnp.bfloat16)


def chip_of():
    me = lax.axis_index("ctx")
    return me % 2, me // 2


def joined_in(doc_ref, chip):
    return (doc_ref[0, 2 * chip] == doc_ref[0, 2 * chip + 1]).astype(F32)


def merge_kernel(block, chips, doc_ref, kept_ref, got_ref, *refs):
    outs, part_ref, chip_ref = refs[:chips], refs[chips], refs[chips + 1]
    core, chip = chip_of()
    first = core == 0
    half = kept_ref.shape[1]
    part = half // chips
    joined = joined_in(doc_ref, chip)
    rate = kept_ref[6]
    part_ref[...] = kept_ref[6, pl.ds(pl.multiple_of(chip * part, part), part), :]
    hop = joined * jnp.exp(-block * rate)
    link = joined * jnp.exp(-rate)
    left = [jnp.where(first, kept_ref[i], got_ref[i]) for i in range(6)]
    right = [jnp.where(first, got_ref[i], kept_ref[i]) for i in range(6)]
    chip_ref[0] = right[0] + hop * left[0]
    chip_ref[1] = right[1] + hop * (left[1] + block * left[0])
    chip_ref[2] = left[2] + hop * right[2]
    chip_ref[3] = left[3] + hop * (right[3] + block * right[2])
    chip_ref[4] = left[4] + right[4] + link * (right[2] * left[0])
    chip_ref[5] = left[5] + right[5] + link * ((right[3] + right[2]) * left[0] + right[2] * left[1])
    for away in range(chips):
        start = pl.multiple_of((chip ^ away) * part, part)
        outs[away][...] = chip_ref[:, pl.ds(start, part), :]


def scan_kernel(block, chips, doc_ref, rate_ref, after_ref, *refs):
    ins, outs, total_ref = refs[:chips], refs[chips : 2 * chips], refs[2 * chips]
    ordered, ends = refs[2 * chips + 1], refs[2 * chips + 2]
    core, chip = chip_of()
    for away in range(chips):
        ordered[chip ^ away] = ins[away][...]
    rate = rate_ref[...]
    lam = jnp.exp(-rate)
    span = 2.0 * block
    hop = jnp.exp(-span * rate)
    zero = jnp.zeros_like(rate)
    state, lag_state, res, grad_lag = zero, zero, zero, zero
    for j in range(chips):
        ends[j, 0] = state
        res = res + (ordered[j, 4] + lam * (ordered[j, 2] * state))
        grad_lag = grad_lag + (
            ordered[j, 5]
            + lam * ((ordered[j, 3] + ordered[j, 2]) * state + ordered[j, 2] * lag_state)
        )
        if j + 1 < chips:
            through = joined_in(doc_ref, j) * hop
            keep = (doc_ref[0, 2 * j + 1] == doc_ref[0, 2 * j + 2]).astype(F32)
            lag_state = keep * (ordered[j, 1] + through * (lag_state + span * state))
            state = keep * (ordered[j, 0] + through * state)
    back = zero
    for j in range(chips - 1, -1, -1):
        ends[j, 1] = back
        if j > 0:
            through = joined_in(doc_ref, j) * hop
            keep = (doc_ref[0, 2 * j - 1] == doc_ref[0, 2 * j]).astype(F32)
            back = keep * (ordered[j, 2] + through * back)
    for away in range(chips):
        outs[away][...] = ends[chip ^ away]
    total_ref[0] = res
    total_ref[1] = grad_lag


def expand_kernel(block, chips, doc_ref, kept_ref, got_ref, after_ref, *refs):
    ins, mine_ref, send_ref, whole = refs[:chips], refs[chips], refs[chips + 1], refs[chips + 2]
    core, chip = chip_of()
    first = core == 0
    joined = joined_in(doc_ref, chip)
    part = ins[0].shape[1]
    for away in range(chips):
        start = pl.multiple_of((chip ^ away) * part, part)
        whole[:, pl.ds(start, part), :] = ins[away][...]
    hop = joined * jnp.exp(-block * kept_ref[6])
    end_left = jnp.where(first, kept_ref[0], got_ref[0])
    head_right = jnp.where(first, got_ref[2], kept_ref[2])
    state, back = whole[0], whole[1]
    state_right = joined * end_left + hop * state
    back_left = joined * head_right + hop * back
    mine_ref[0] = jnp.where(first, state, state_right)
    mine_ref[1] = jnp.where(first, back_left, back)
    send_ref[0] = jnp.where(first, state_right, state)
    send_ref[1] = jnp.where(first, back, back_left)


def gather_kernel(chips, zeros_ref, *refs):
    ins, out_ref = refs[:chips], refs[chips]
    core, chip = chip_of()
    part = ins[0].shape[1]
    for away in range(chips):
        start = pl.multiple_of((chip ^ away) * part, part)
        out_ref[:, pl.ds(start, part), :] = ins[away][...]


def final_kernel(scale, rate_ref, residue_ref, kept_ref, got_ref, res_ref, grad_ref, sums, res_rows, grad_rows):
    core, chip = chip_of()
    half = kept_ref.shape[1]
    sums[:, pl.ds(pl.multiple_of(core * half, half), half), :] = kept_ref[...]
    sums[:, pl.ds(pl.multiple_of((1 - core) * half, half), half), :] = got_ref[...]
    modes, channels = residue_ref.shape
    tall = channels // LANES
    for group in range(channels // GROUP):
        for m in range(modes):
            window = pl.ds(m * tall + group * SUBS, SUBS)
            rate = rate_ref[window, :]
            root = jnp.sqrt(2.0 * rate) * scale
            grad_res, grad_lag = sums[0, window, :], sums[1, window, :]
            target = pl.ds((m // 8) * 64 + m % 8, 8, stride=8)
            res_rows[target, :] = root * grad_res
            grad_rows[target, :] = root * (0.5 * grad_res - rate * grad_lag)
        for eight in range(modes // 8):
            for tile in range(SUBS):
                place = (pl.ds(eight * 8, 8), pl.ds(group * GROUP + tile * LANES, LANES))
                rows = pl.ds(eight * 64 + tile * 8, 8)
                res_ref[place] = res_rows[rows, :]
                grad_ref[place] = residue_ref[place] * grad_rows[rows, :]


def whole(array):
    rank = len(array.shape)
    return pl.BlockSpec(array.shape, lambda i: (0,) * rank)


def small_call(kernel, name, ins, outs, scratch):
    return pl.pallas_call(
        kernel,
        grid=(1,),
        in_specs=[scalar_spec() if x.dtype == jnp.int32 else whole(x) for x in ins],
        out_specs=[whole(x) for x in outs],
        out_shape=outs,
        scratch_shapes=scratch,
        compiler_params=params(),
        name=name,
    )(*ins)


def f32(*shape):
    return jax.ShapeDtypeStruct(shape, F32)


def scalar_spec():
    return pl.BlockSpec(memory_space=pltpu.SMEM)


def params(mib=16):
    return pltpu.CompilerParams(vmem_limit_bytes=mib * 1024 * 1024)


def body(q_proj, k_proj, v_proj, out_grad, residue, pole_decay, group_doc):
    block, channels = q_proj.shape[1], q_proj.shape[2]
    modes = residue.shape[0]
    n_ctx, n_dp = lax.axis_size("ctx"), lax.axis_size("dp")
    row_len = block * n_ctx
    total_tokens = row_len * n_dp
    chips = n_ctx // 2
    groups = channels // GROUP
    chunks = block // CHUNK
    tall = channels // LANES
    rows = modes * tall
    half = rows // 2
    part = half // chips
    halves = modes // 2

    k_in, v_in, q_in, g_in = (x.reshape(block, channels) for x in (k_proj, v_proj, q_proj, out_grad))
    row_scratch = pltpu.VMEM((block * SUBS, LANES), F32)
    mode_scratch = pltpu.VMEM((modes, SUBS, LANES), F32)
    flat_scratch = pltpu.VMEM((modes * SUBS, LANES), F32)
    tap_scratch = pltpu.VMEM((CHUNK, SUBS, LANES), F32)

    def specs(at):
        return (
            pl.BlockSpec((block, GROUP), lambda i: (0, at(i))),
            pl.BlockSpec((modes, SUBS, LANES), lambda i: (0, at(i), 0)),
            pl.BlockSpec((modes, GROUP), lambda i: (0, at(i))),
            pl.BlockSpec((chunks, modes, SUBS, LANES), lambda i: (0, 0, at(i), 0)),
            lambda count: pl.BlockSpec((count, halves, SUBS, LANES), lambda i: (0, 0, at(i), 0)),
        )

    wide, slim, natural, chunked, halved = specs(lambda i: i)
    ends, heads, rate, kept, send = pl.pallas_call(
        partial(stats_kernel, float(row_len)),
        grid=(groups,),
        in_specs=[wide] * 4 + [natural],
        out_specs=[chunked, chunked, slim, halved(7), halved(6)],
        out_shape=[
            jax.ShapeDtypeStruct((chunks, modes, tall, LANES), F32),
            jax.ShapeDtypeStruct((chunks, modes, tall, LANES), F32),
            jax.ShapeDtypeStruct((modes, tall, LANES), F32),
            jax.ShapeDtypeStruct((7, halves, tall, LANES), F32),
            jax.ShapeDtypeStruct((6, halves, tall, LANES), F32),
        ],
        scratch_shapes=[row_scratch] * 2 + [flat_scratch] + [mode_scratch] * 11 + [tap_scratch],
        compiler_params=params(BIG),
        name="block_stats",
    )(k_in, v_in, q_in, g_in, pole_decay)

    rate_rows = rate.reshape(rows, LANES)
    kept = kept.reshape(7, half, LANES)
    send = send.reshape(6, half, LANES)

    def swap_core(x):
        return lax.ppermute(x, "ctx", [(i, i ^ 1) for i in range(n_ctx)])

    def swap_chips(xs):
        return [xs[0]] + [
            lax.ppermute(xs[away], "ctx", [(i, i ^ (2 * away)) for i in range(n_ctx)]) for away in range(1, chips)
        ]

    got = swap_core(send)
    *pieces, rate_part = small_call(
        partial(merge_kernel, float(block), chips),
        "chip_stats",
        [group_doc, kept, got],
        [f32(6, part, LANES)] * chips + [f32(part, LANES)],
        [pltpu.VMEM((6, half, LANES), F32)],
    )
    columns = pl.BlockSpec((1, block, SUBS, LANES), lambda i: (i, 0, 0, 0))
    z_local, w_local, zeros = pl.pallas_call(
        local_kernel,
        grid=(groups,),
        in_specs=[wide] * 4 + [slim, natural] + [chunked] * 2 + [pl.BlockSpec(memory_space=pl.ANY)],
        out_specs=[columns] * 2 + [pl.BlockSpec((1, LANES), lambda i: (0, 0))],
        out_shape=[f32(groups, block, SUBS, LANES)] * 2 + [f32(1, LANES)],
        scratch_shapes=[row_scratch] * 2 + [flat_scratch] + [mode_scratch] * 5 + [tap_scratch],
        compiler_params=params(BIG),
        cost_estimate=pl.CostEstimate(flops=10_000_000_000, bytes_accessed=20_000_000, transcendentals=0),
        name="local_outputs",
    )(k_in, v_in, q_in, g_in, rate, residue, ends, heads, rate_part)
    scanned = small_call(
        partial(scan_kernel, float(block), chips),
        "row_scan",
        [group_doc, rate_part, zeros, *swap_chips(pieces)],
        [f32(2, part, LANES)] * (chips + 1),
        [pltpu.VMEM((chips, 6, part, LANES), F32), pltpu.VMEM((chips, 2, part, LANES), F32)],
    )
    total, reach, outs, done = scanned[chips], 1, [], 0
    arrived = swap_chips(scanned[:chips])
    if n_dp > 2:
        total = total + lax.ppermute(total, "dp", [(i, i ^ reach) for i in range(n_dp)])
        reach *= 2
    mine, give = small_call(
        partial(expand_kernel, float(block), chips),
        "block_edges",
        [group_doc, kept, got, total, *arrived],
        [f32(2, half, LANES)] * 2,
        [pltpu.VMEM((2, half, LANES), F32)],
    )
    theirs = swap_core(give)
    edges = [x.reshape(2, halves, tall, LANES) for x in (mine, theirs)]

    def outputs(first, count, after, outs):
        wide, slim, natural, chunked, halved = specs(lambda i: i + first)
        columns = pl.BlockSpec((1, block, SUBS, LANES), lambda i: (i + first, 0, 0, 0))
        result = pl.pallas_call(
            partial(output_kernel, len(outs)),
            grid=(count,),
            in_specs=[wide] * 4 + [slim, natural] + [columns] * 2 + [halved(2)] * 2
            + [pl.BlockSpec(memory_space=pl.ANY)] * (1 + len(outs)),
            out_specs=[wide] * 4 + [pl.BlockSpec((1, LANES), lambda i: (0, 0))],
            out_shape=[jax.ShapeDtypeStruct((block, channels), jnp.bfloat16)] * 4 + [f32(1, LANES)],
            input_output_aliases={11 + i: i for i in range(len(outs))},
            scratch_shapes=[row_scratch] * 2 + [flat_scratch] + [mode_scratch] * 3,
            compiler_params=params(BIG),
            cost_estimate=pl.CostEstimate(
                flops=2_000_000_000 * count, bytes_accessed=5_000_000 * count, transcendentals=0
            ),
            name="outputs",
        )(k_in, v_in, q_in, g_in, rate, residue, z_local, w_local, *edges, after, *outs)
        return result[:4], result[4]

    while reach < n_dp:
        other = lax.ppermute(total, "dp", [(i, i ^ reach) for i in range(n_dp)])
        reach *= 2
        if reach >= n_dp and groups > 1:
            done = groups // 2
            outs, zeros = outputs(0, done, total, outs)
            other = other + zeros
        total = total + other
    sums = swap_chips([total] * chips)
    outs, zeros = outputs(done, groups - done, total, outs)
    (gathered,) = small_call(
        partial(gather_kernel, chips), "gather_sums", [zeros, *sums], [f32(2, half, LANES)], []
    )
    residue_grad, pole_grad = small_call(
        partial(final_kernel, 1.0 / math.sqrt(total_tokens)),
        "parameter_grads",
        [rate_rows, residue, gathered, swap_core(gathered)],
        [f32(modes, channels)] * 2,
        [pltpu.VMEM((2, rows, LANES), F32)] + [flat_scratch] * 2,
    )
    return (*(x[None] for x in outs), residue_grad, pole_grad)


def solution(mesh):
    tokens = P("dp", "ctx", None)
    return jax.shard_map(
        body,
        mesh=mesh,
        in_specs=(tokens, tokens, tokens, tokens, P(), P(), P("dp", None)),
        out_specs=(tokens, tokens, tokens, tokens, P(), P()),
        check_vma=False,
    )
```

```python
from functools import partial
import math

import jax
import jax.numpy as jnp
from jax import lax
from jax.experimental import pallas as pl
from jax.experimental.pallas import tpu as pltpu
from jax.sharding import PartitionSpec as P

F32 = jnp.float32
LANES = 128
SUBS = 8
GROUP = LANES * SUBS
CHUNK = 8
BIG = 32


def to_rows(left_ref, right_ref, rows_ref):
    tokens = left_ref.shape[0]
    for pair in range(tokens // 16):
        window = pl.ds(pair * 16, 16)
        for tile in range(SUBS):
            lanes = pl.ds(tile * LANES, LANES)
            product = left_ref[window, lanes].astype(F32) * right_ref[window, lanes].astype(F32)
            for part in range(2):
                start = (pair * 2 + part) * 64 + tile * 8
                rows_ref[pl.ds(start, 8), :] = product[part * 8 : part * 8 + 8]


def token_row(rows_ref, chunk, token):
    return rows_ref[pl.ds(chunk * 64 + token, 8, stride=8), :]


def mode_rows(natural_ref, rows_ref):
    for eight in range(natural_ref.shape[0] // 8):
        for tile in range(SUBS):
            rows_ref[pl.ds(eight * 64 + tile * 8, 8), :] = natural_ref[
                pl.ds(eight * 8, 8), pl.ds(tile * LANES, LANES)
            ]


def mode_row(rows_ref, mode):
    return rows_ref[pl.ds((mode // 8) * 64 + mode % 8, 8, stride=8), :]


def stats_kernel(
    row_len, k_ref, v_ref, q_ref, g_ref, pole_ref, c_ref, b_ref, rate_ref, kept_ref, send_ref,
    u_rows, d_rows, p_rows, lam_s, jump_s, slope_s, state_s, lag_s, res_s, mixl_s, head_s, headl_s, headm_s, pow_s,
    corr_s,
):
    modes = pole_ref.shape[0]
    chunks = k_ref.shape[0] // CHUNK
    first = lax.axis_index("ctx") % 2 == 0
    to_rows(k_ref, v_ref, u_rows)
    to_rows(g_ref, q_ref, d_rows)
    mode_rows(pole_ref, p_rows)
    zero = jnp.zeros((SUBS, LANES), F32)
    for m in range(modes):
        rate = mode_row(p_rows, m) / row_len
        rate_ref[0, m] = rate
        lam = jnp.exp(-rate)
        square = lam * lam
        fourth = square * square
        lam_s[m] = lam
        jump_s[m] = fourth * fourth
        slope_s[m] = CHUNK * (fourth * (square * lam))
        for ref in (state_s, lag_s, res_s, mixl_s, head_s, headl_s, headm_s):
            ref[m] = zero
        pow_s[m] = zero + 1.0
    for lag in range(CHUNK):
        corr_s[lag] = zero

    def step(chunk, _):
        u = [token_row(u_rows, chunk, t) for t in range(CHUNK)]
        d = [token_row(d_rows, chunk, t) for t in range(CHUNK)]
        for lag in range(CHUNK):
            total = corr_s[lag]
            for t in range(CHUNK - lag):
                total = total + d[t + lag] * u[t]
            corr_s[lag] = total
        offset = (chunk * CHUNK).astype(F32)
        for m in range(modes):
            lam = lam_s[m]
            end, endl = u[0], None
            for t in range(1, CHUNK):
                endl = end if endl is None else endl * lam + end
                end = end * lam + u[t]
            head, headl = d[CHUNK - 1], None
            for t in range(CHUNK - 2, -1, -1):
                headl = head if headl is None else headl * lam + head
                head = head * lam + d[t]
            c_ref[0, chunk, m] = end
            b_ref[0, chunk, m] = head
            state, lag_state = state_s[m], lag_s[m]
            res_s[m] = res_s[m] + head * state
            mixl_s[m] = mixl_s[m] + (headl * state + head * lag_state)
            jump = jump_s[m]
            lag_s[m] = lag_state * jump + (state * slope_s[m] + endl)
            state_s[m] = state * jump + end
            power = pow_s[m]
            far = power * head
            head_s[m] = head_s[m] + far
            headl_s[m] = headl_s[m] + power * headl
            headm_s[m] = headm_s[m] + offset * far
            pow_s[m] = power * jump
        return 0

    lax.fori_loop(0, chunks, step, 0)
    def stats_of(m):
        lam = lam_s[m]
        near, nearl = corr_s[CHUNK - 1], None
        for lag in range(CHUNK - 2, -1, -1):
            nearl = near if nearl is None else nearl * lam + near
            near = near * lam + corr_s[lag]
        res = res_s[m]
        return (
            state_s[m],
            lam * lag_s[m],
            head_s[m],
            lam * headl_s[m] + headm_s[m],
            near + lam * res,
            lam * (nearl + (res + lam * mixl_s[m])),
        )

    half = modes // 2
    for m in range(half):
        kept_ref[6, 0, m] = jnp.where(first, rate_ref[0, m], rate_ref[0, m + half])
        for i, (low, high) in enumerate(zip(stats_of(m), stats_of(m + half))):
            kept_ref[i, 0, m] = jnp.where(first, low, high)
            send_ref[i, 0, m] = jnp.where(first, high, low)


def local_kernel(
    k_ref, v_ref, q_ref, g_ref, rate_ref, residue_ref, c_ref, b_ref, after_ref,
    z_ref, w_ref, zeros_ref, u_rows, d_rows, r_rows, lam_s, jump_s, lead_s, state_s, back_s, tap_s,
):
    modes = rate_ref.shape[1]
    chunks = k_ref.shape[0] // CHUNK
    zeros_ref[...] = jnp.zeros((1, LANES), F32)
    to_rows(k_ref, v_ref, u_rows)
    to_rows(g_ref, q_ref, d_rows)
    mode_rows(residue_ref, r_rows)
    zero = jnp.zeros((SUBS, LANES), F32)
    taps = [zero for _ in range(CHUNK)]
    for m in range(modes):
        rate = rate_ref[0, m]
        lam = jnp.exp(-rate)
        square = lam * lam
        fourth = square * square
        lam_s[m] = lam
        jump_s[m] = fourth * fourth
        power = mode_row(r_rows, m) * jnp.sqrt(2.0 * rate)
        lead_s[m] = power * lam
        for lag in range(CHUNK):
            taps[lag] = taps[lag] + power
            power = power * lam
        state_s[m] = zero
        back_s[m] = zero
    for lag in range(CHUNK):
        tap_s[lag] = taps[lag]

    def step(chunk, _):
        mirror = chunks - 1 - chunk
        u = [token_row(u_rows, chunk, t) for t in range(CHUNK)]
        z = [None] * CHUNK
        for lag in range(CHUNK):
            tap = tap_s[lag]
            for t in range(lag, CHUNK):
                term = tap * u[t - lag]
                z[t] = term if z[t] is None else z[t] + term
        d = [token_row(d_rows, mirror, t) for t in range(CHUNK)]
        w = [None] * CHUNK
        for lag in range(CHUNK):
            tap = tap_s[lag]
            for t in range(CHUNK - lag):
                term = tap * d[t + lag]
                w[t] = term if w[t] is None else w[t] + term
        for m in range(modes):
            lam, lead, jump = lam_s[m], lead_s[m], jump_s[m]
            state, back = state_s[m], back_s[m]
            ahead, behind = state * lead, back * lead
            for t in range(CHUNK):
                z[t] = z[t] + ahead
                w[CHUNK - 1 - t] = w[CHUNK - 1 - t] + behind
                if t + 1 < CHUNK:
                    ahead = ahead * lam
                    behind = behind * lam
            state_s[m] = state * jump + c_ref[0, chunk, m]
            back_s[m] = back * jump + b_ref[0, mirror, m]
        for t in range(CHUNK):
            z_ref[0, chunk * CHUNK + t] = z[t]
            w_ref[0, mirror * CHUNK + t] = w[t]
        return 0

    lax.fori_loop(0, chunks, step, 0)


def output_kernel(
    earlier, k_ref, v_ref, q_ref, g_ref, rate_ref, residue_ref, zl_ref, wl_ref, kept_ref, got_ref, after_ref, *refs
):
    mixed_ref, qg_ref, kg_ref, vg_ref, zeros_ref = refs[earlier : earlier + 5]
    z_rows, w_rows, r_rows, lam_s, ahead_s, behind_s = refs[earlier + 5 :]
    modes = rate_ref.shape[1]
    half = modes // 2
    chunks = k_ref.shape[0] // CHUNK
    first = lax.axis_index("ctx") % 2 == 0
    zeros_ref[...] = jnp.zeros((1, LANES), F32)
    mode_rows(residue_ref, r_rows)
    for m in range(modes):
        rate = rate_ref[0, m]
        lam = jnp.exp(-rate)
        lam_s[m] = lam
        lead = mode_row(r_rows, m) * jnp.sqrt(2.0 * rate) * lam
        mine = first if m < half else jnp.logical_not(first)
        ahead_s[m] = lead * jnp.where(mine, kept_ref[0, 0, m % half], got_ref[0, 0, m % half])
        behind_s[m] = lead * jnp.where(mine, kept_ref[1, 0, m % half], got_ref[1, 0, m % half])

    def step(chunk, _):
        mirror = chunks - 1 - chunk
        z = [zl_ref[0, chunk * CHUNK + t] for t in range(CHUNK)]
        w = [wl_ref[0, mirror * CHUNK + t] for t in range(CHUNK)]
        for m in range(modes):
            lam = lam_s[m]
            ahead, behind = ahead_s[m], behind_s[m]
            for t in range(CHUNK):
                z[t] = z[t] + ahead
                ahead = ahead * lam
                w[CHUNK - 1 - t] = w[CHUNK - 1 - t] + behind
                behind = behind * lam
            ahead_s[m] = ahead
            behind_s[m] = behind
        for t in range(CHUNK):
            z_rows[pl.ds(chunk * 64 + t, 8, stride=8), :] = z[t]
            w_rows[pl.ds(mirror * 64 + t, 8, stride=8), :] = w[t]
        return 0

    lax.fori_loop(0, chunks, step, 0)
    for pair in range(chunks // 2):
        window = pl.ds(pair * 16, 16)
        for tile in range(SUBS):
            lanes = pl.ds(tile * LANES, LANES)
            z = jnp.concatenate([z_rows[pl.ds((pair * 2 + part) * 64 + tile * 8, 8), :] for part in range(2)], axis=0)
            w = jnp.concatenate([w_rows[pl.ds((pair * 2 + part) * 64 + tile * 8, 8), :] for part in range(2)], axis=0)
            mixed_ref[window, lanes] = (q_ref[window, lanes].astype(F32) * z).astype(jnp.bfloat16)
            qg_ref[window, lanes] = (g_ref[window, lanes].astype(F32) * z).astype(jnp.bfloat16)
            kg_ref[window, lanes] = (w * v_ref[window, lanes].astype(F32)).astype(jnp.bfloat16)
            vg_ref[window, lanes] = (w * k_ref[window, lanes].astype(F32)).astype(jnp.bfloat16)


def chip_of():
    me = lax.axis_index("ctx")
    return me % 2, me // 2


def joined_in(doc_ref, chip):
    return (doc_ref[0, 2 * chip] == doc_ref[0, 2 * chip + 1]).astype(F32)


def merge_kernel(block, chips, doc_ref, kept_ref, got_ref, *refs):
    outs, part_ref, chip_ref = refs[:chips], refs[chips], refs[chips + 1]
    core, chip = chip_of()
    first = core == 0
    half = kept_ref.shape[1]
    part = half // chips
    joined = joined_in(doc_ref, chip)
    rate = kept_ref[6]
    part_ref[...] = kept_ref[6, pl.ds(pl.multiple_of(chip * part, part), part), :]
    hop = joined * jnp.exp(-block * rate)
    link = joined * jnp.exp(-rate)
    left = [jnp.where(first, kept_ref[i], got_ref[i]) for i in range(6)]
    right = [jnp.where(first, got_ref[i], kept_ref[i]) for i in range(6)]
    chip_ref[0] = right[0] + hop * left[0]
    chip_ref[1] = right[1] + hop * (left[1] + block * left[0])
    chip_ref[2] = left[2] + hop * right[2]
    chip_ref[3] = left[3] + hop * (right[3] + block * right[2])
    chip_ref[4] = left[4] + right[4] + link * (right[2] * left[0])
    chip_ref[5] = left[5] + right[5] + link * ((right[3] + right[2]) * left[0] + right[2] * left[1])
    for away in range(chips):
        start = pl.multiple_of((chip ^ away) * part, part)
        outs[away][...] = chip_ref[:, pl.ds(start, part), :]


def scan_kernel(block, chips, doc_ref, rate_ref, *refs):
    refs = refs[:chips] + refs[chips + 1 :]
    ins, outs, total_ref = refs[:chips], refs[chips : 2 * chips], refs[2 * chips]
    ordered, ends = refs[2 * chips + 1], refs[2 * chips + 2]
    core, chip = chip_of()
    for away in range(chips):
        ordered[chip ^ away] = ins[away][...]
    rate = rate_ref[...]
    lam = jnp.exp(-rate)
    span = 2.0 * block
    hop = jnp.exp(-span * rate)
    zero = jnp.zeros_like(rate)
    state, lag_state, res, grad_lag = zero, zero, zero, zero
    for j in range(chips):
        ends[j, 0] = state
        res = res + (ordered[j, 4] + lam * (ordered[j, 2] * state))
        grad_lag = grad_lag + (
            ordered[j, 5]
            + lam * ((ordered[j, 3] + ordered[j, 2]) * state + ordered[j, 2] * lag_state)
        )
        if j + 1 < chips:
            through = joined_in(doc_ref, j) * hop
            keep = (doc_ref[0, 2 * j + 1] == doc_ref[0, 2 * j + 2]).astype(F32)
            lag_state = keep * (ordered[j, 1] + through * (lag_state + span * state))
            state = keep * (ordered[j, 0] + through * state)
    back = zero
    for j in range(chips - 1, -1, -1):
        ends[j, 1] = back
        if j > 0:
            through = joined_in(doc_ref, j) * hop
            keep = (doc_ref[0, 2 * j - 1] == doc_ref[0, 2 * j]).astype(F32)
            back = keep * (ordered[j, 2] + through * back)
    for away in range(chips):
        outs[away][...] = ends[chip ^ away]
    total_ref[0] = res
    total_ref[1] = grad_lag


def expand_kernel(block, chips, doc_ref, kept_ref, got_ref, *refs):
    ins, mine_ref, send_ref, whole = refs[:chips], refs[chips], refs[chips + 1], refs[chips + 2]
    core, chip = chip_of()
    first = core == 0
    joined = joined_in(doc_ref, chip)
    part = ins[0].shape[1]
    for away in range(chips):
        start = pl.multiple_of((chip ^ away) * part, part)
        whole[:, pl.ds(start, part), :] = ins[away][...]
    hop = joined * jnp.exp(-block * kept_ref[6])
    end_left = jnp.where(first, kept_ref[0], got_ref[0])
    head_right = jnp.where(first, got_ref[2], kept_ref[2])
    state, back = whole[0], whole[1]
    state_right = joined * end_left + hop * state
    back_left = joined * head_right + hop * back
    mine_ref[0] = jnp.where(first, state, state_right)
    mine_ref[1] = jnp.where(first, back_left, back)
    send_ref[0] = jnp.where(first, state_right, state)
    send_ref[1] = jnp.where(first, back, back_left)


def gather_kernel(chips, *refs):
    ins, out_ref = refs[:chips], refs[chips + 1]
    core, chip = chip_of()
    part = ins[0].shape[1]
    for away in range(chips):
        start = pl.multiple_of((chip ^ away) * part, part)
        out_ref[:, pl.ds(start, part), :] = ins[away][...]


def final_kernel(scale, rate_ref, residue_ref, kept_ref, got_ref, res_ref, grad_ref, sums, res_rows, grad_rows):
    core, chip = chip_of()
    half = kept_ref.shape[1]
    sums[:, pl.ds(pl.multiple_of(core * half, half), half), :] = kept_ref[...]
    sums[:, pl.ds(pl.multiple_of((1 - core) * half, half), half), :] = got_ref[...]
    modes, channels = residue_ref.shape
    halves = modes // 2
    for group in range(channels // GROUP):
        for m in range(modes):
            window = pl.ds((m // halves) * half + (group * halves + m % halves) * SUBS, SUBS)
            rate = rate_ref[group, m]
            root = jnp.sqrt(2.0 * rate) * scale
            grad_res, grad_lag = sums[0, window, :], sums[1, window, :]
            target = pl.ds((m // 8) * 64 + m % 8, 8, stride=8)
            res_rows[target, :] = root * grad_res
            grad_rows[target, :] = root * (0.5 * grad_res - rate * grad_lag)
        for eight in range(modes // 8):
            for tile in range(SUBS):
                place = (pl.ds(eight * 8, 8), pl.ds(group * GROUP + tile * LANES, LANES))
                rows = pl.ds(eight * 64 + tile * 8, 8)
                res_ref[place] = res_rows[rows, :]
                grad_ref[place] = residue_ref[place] * grad_rows[rows, :]


def whole(array):
    rank = len(array.shape)
    return pl.BlockSpec(array.shape, lambda i: (0,) * rank)


def unread():
    return pl.BlockSpec(memory_space=pl.ANY)


def small_call(kernel, name, ins, outs, scratch, after=()):
    return pl.pallas_call(
        kernel,
        grid=(1,),
        in_specs=[scalar_spec() if x.dtype == jnp.int32 else whole(x) for x in ins] + [unread() for _ in after],
        out_specs=[whole(x) for x in outs],
        out_shape=outs,
        scratch_shapes=scratch,
        compiler_params=params(),
        name=name,
    )(*ins, *after)


def hbm(x):
    return pltpu.with_memory_space_constraint(x, pltpu.HBM)


def vmem(x):
    return pltpu.with_memory_space_constraint(x, pltpu.VMEM)


def f32(*shape):
    return jax.ShapeDtypeStruct(shape, F32)


def scalar_spec():
    return pl.BlockSpec(memory_space=pltpu.SMEM)


def params(mib=16):
    return pltpu.CompilerParams(vmem_limit_bytes=mib * 1024 * 1024)


def body(q_proj, k_proj, v_proj, out_grad, residue, pole_decay, group_doc):
    block, channels = q_proj.shape[1], q_proj.shape[2]
    modes = residue.shape[0]
    n_ctx, n_dp = lax.axis_size("ctx"), lax.axis_size("dp")
    row_len = block * n_ctx
    total_tokens = row_len * n_dp
    chips = n_ctx // 2
    groups = channels // GROUP
    chunks = block // CHUNK
    rows = modes * channels // LANES
    half = rows // 2
    part = half // chips
    halves = modes // 2

    k_in, v_in, q_in, g_in = (hbm(x.reshape(block, channels)) for x in (k_proj, v_proj, q_proj, out_grad))
    row_scratch = pltpu.VMEM((block * SUBS, LANES), F32)
    mode_scratch = pltpu.VMEM((modes, SUBS, LANES), F32)
    flat_scratch = pltpu.VMEM((modes * SUBS, LANES), F32)
    tap_scratch = pltpu.VMEM((CHUNK, SUBS, LANES), F32)

    def specs(at):
        return (
            pl.BlockSpec((block, GROUP), lambda i: (0, at(i))),
            pl.BlockSpec((1, modes, SUBS, LANES), lambda i: (at(i), 0, 0, 0)),
            pl.BlockSpec((modes, GROUP), lambda i: (0, at(i))),
            pl.BlockSpec((1, chunks, modes, SUBS, LANES), lambda i: (at(i), 0, 0, 0, 0)),
            lambda count: pl.BlockSpec((count, 1, halves, SUBS, LANES), lambda i: (0, at(i), 0, 0, 0)),
        )

    wide, slim, natural, chunked, halved = specs(lambda i: i)
    ends, heads, rate, kept, send = pl.pallas_call(
        partial(stats_kernel, float(row_len)),
        grid=(groups,),
        in_specs=[wide] * 4 + [natural],
        out_specs=[chunked, chunked, slim, halved(7), halved(6)],
        out_shape=[
            pltpu.VMEM((groups, chunks, modes, SUBS, LANES), F32),
            pltpu.VMEM((groups, chunks, modes, SUBS, LANES), F32),
            pltpu.HBM((groups, modes, SUBS, LANES), F32),
            pltpu.VMEM((7, groups, halves, SUBS, LANES), F32),
            pltpu.VMEM((6, groups, halves, SUBS, LANES), F32),
        ],
        scratch_shapes=[row_scratch] * 2 + [flat_scratch] + [mode_scratch] * 11 + [tap_scratch],
        compiler_params=params(BIG),
        name="block_stats",
    )(k_in, v_in, q_in, g_in, hbm(pole_decay))

    kept = kept.reshape(7, half, LANES)
    send = send.reshape(6, half, LANES)

    def swap_core(x):
        return lax.ppermute(x, "ctx", [(i, i ^ 1) for i in range(n_ctx)])

    def swap_chips(xs):
        return [xs[0]] + [
            lax.ppermute(xs[away], "ctx", [(i, i ^ (2 * away)) for i in range(n_ctx)]) for away in range(1, chips)
        ]

    got = swap_core(send)
    *pieces, rate_part = small_call(
        partial(merge_kernel, float(block), chips),
        "chip_stats",
        [group_doc, kept, got],
        [f32(6, part, LANES)] * chips + [f32(part, LANES)],
        [pltpu.VMEM((6, half, LANES), F32)],
    )
    columns = pl.BlockSpec((1, block, SUBS, LANES), lambda i: (i, 0, 0, 0))
    z_local, w_local, zeros = pl.pallas_call(
        local_kernel,
        grid=(groups,),
        in_specs=[wide] * 4 + [slim, natural] + [chunked] * 2 + [pl.BlockSpec(memory_space=pl.ANY)],
        out_specs=[columns] * 2 + [pl.BlockSpec((1, LANES), lambda i: (0, 0))],
        out_shape=[pltpu.VMEM((groups, block, SUBS, LANES), F32)] * 2 + [pltpu.HBM((1, LANES), F32)],
        scratch_shapes=[row_scratch] * 2 + [flat_scratch] + [mode_scratch] * 5 + [tap_scratch],
        compiler_params=params(BIG),
        cost_estimate=pl.CostEstimate(flops=10_000_000_000, bytes_accessed=20_000_000, transcendentals=0),
        name="local_outputs",
    )(k_in, v_in, q_in, g_in, hbm(rate), hbm(residue), vmem(ends), vmem(heads), rate_part)
    scanned = small_call(
        partial(scan_kernel, float(block), chips),
        "row_scan",
        [group_doc, rate_part, *swap_chips(pieces)],
        [f32(2, part, LANES)] * (chips + 1),
        [pltpu.VMEM((chips, 6, part, LANES), F32), pltpu.VMEM((chips, 2, part, LANES), F32)],
        after=[hbm(zeros)],
    )
    total = scanned[chips]
    for away in [lax.ppermute(total, "dp", [(i, i ^ away) for i in range(n_dp)]) for away in range(1, n_dp)]:
        total = total + away
    mine, give = small_call(
        partial(expand_kernel, float(block), chips),
        "block_edges",
        [group_doc, kept, got, *swap_chips(scanned[:chips])],
        [f32(2, half, LANES)] * 2,
        [pltpu.VMEM((2, half, LANES), F32)],
    )
    theirs = swap_core(give)

    edges = [x.reshape(2, groups, halves, SUBS, LANES) for x in (mine, theirs)]

    def outputs(first, count, after, outs):
        wide, slim, natural, chunked, halved = specs(lambda i: i + first)
        columns = pl.BlockSpec((1, block, SUBS, LANES), lambda i: (i + first, 0, 0, 0))
        result = pl.pallas_call(
            partial(output_kernel, len(outs)),
            grid=(count,),
            in_specs=[wide] * 4 + [slim, natural] + [columns] * 2 + [halved(2)] * 2
            + [pl.BlockSpec(memory_space=pl.ANY)] * (1 + len(outs)),
            out_specs=[wide] * 4 + [pl.BlockSpec((1, LANES), lambda i: (0, 0))],
            out_shape=[pltpu.HBM((block, channels), jnp.bfloat16)] * 4 + [pltpu.HBM((1, LANES), F32)],
            input_output_aliases={11 + i: i for i in range(len(outs))},
            scratch_shapes=[row_scratch] * 2 + [flat_scratch] + [mode_scratch] * 3,
            compiler_params=params(BIG),
            cost_estimate=pl.CostEstimate(
                flops=100_000_000 * count, bytes_accessed=500_000 * count, transcendentals=0
            ),
            name="outputs",
        )(k_in, v_in, q_in, g_in, hbm(rate), hbm(residue), vmem(z_local), vmem(w_local), *edges, after, *outs)
        return result[:4], result[4]

    sums = swap_chips([total] * chips)
    outs, zeros = outputs(0, (groups + 1) // 2, total, [])
    (gathered,) = small_call(
        partial(gather_kernel, chips), "gather_sums", sums, [f32(2, half, LANES)], [], after=[hbm(zeros)]
    )
    if groups > 1:
        outs, _ = outputs((groups + 1) // 2, groups // 2, gathered, outs)
    residue_grad, pole_grad = small_call(
        partial(final_kernel, 1.0 / math.sqrt(total_tokens)),
        "parameter_grads",
        [rate, residue, gathered, swap_core(gathered)],
        [f32(modes, channels)] * 2,
        [pltpu.VMEM((2, rows, LANES), F32)] + [flat_scratch] * 2,
    )
    return (*(x[None] for x in outs), residue_grad, pole_grad)


def solution(mesh):
    tokens = P("dp", "ctx", None)
    return jax.shard_map(
        body,
        mesh=mesh,
        in_specs=(tokens, tokens, tokens, tokens, P(), P(), P("dp", None)),
        out_specs=(tokens, tokens, tokens, tokens, P(), P()),
        check_vma=False,
    )
```

```python
from functools import partial
import math

import jax
import jax.numpy as jnp
from jax import lax
from jax.experimental import pallas as pl
from jax.experimental.pallas import tpu as pltpu
from jax.sharding import PartitionSpec as P

F32 = jnp.float32
LANES = 128
SUBS = 8
GROUP = LANES * SUBS
CHUNK = 8
BIG = 32


def to_rows(left_ref, right_ref, rows_ref):
    tokens = left_ref.shape[0]
    for pair in range(tokens // 16):
        window = pl.ds(pair * 16, 16)
        for tile in range(SUBS):
            lanes = pl.ds(tile * LANES, LANES)
            product = left_ref[window, lanes].astype(F32) * right_ref[window, lanes].astype(F32)
            for part in range(2):
                start = (pair * 2 + part) * 64 + tile * 8
                rows_ref[pl.ds(start, 8), :] = product[part * 8 : part * 8 + 8]


def token_row(rows_ref, chunk, token):
    return rows_ref[pl.ds(chunk * 64 + token, 8, stride=8), :]


def mode_rows(natural_ref, rows_ref):
    for eight in range(natural_ref.shape[0] // 8):
        for tile in range(SUBS):
            rows_ref[pl.ds(eight * 64 + tile * 8, 8), :] = natural_ref[
                pl.ds(eight * 8, 8), pl.ds(tile * LANES, LANES)
            ]


def mode_row(rows_ref, mode):
    return rows_ref[pl.ds((mode // 8) * 64 + mode % 8, 8, stride=8), :]


def stats_kernel(
    row_len, k_ref, v_ref, q_ref, g_ref, pole_ref, c_ref, b_ref, rate_ref, kept_ref, send_ref,
    u_rows, d_rows, p_rows, lam_s, jump_s, slope_s, state_s, lag_s, res_s, mixl_s, head_s, headl_s, headm_s, pow_s,
    corr_s,
):
    modes = pole_ref.shape[0]
    chunks = k_ref.shape[0] // CHUNK
    first = lax.axis_index("ctx") % 2 == 0
    to_rows(k_ref, v_ref, u_rows)
    to_rows(g_ref, q_ref, d_rows)
    mode_rows(pole_ref, p_rows)
    zero = jnp.zeros((SUBS, LANES), F32)
    for m in range(modes):
        rate = mode_row(p_rows, m) / row_len
        rate_ref[0, m] = rate
        lam = jnp.exp(-rate)
        square = lam * lam
        fourth = square * square
        lam_s[m] = lam
        jump_s[m] = fourth * fourth
        slope_s[m] = CHUNK * (fourth * (square * lam))
        for ref in (state_s, lag_s, res_s, mixl_s, head_s, headl_s, headm_s):
            ref[m] = zero
        pow_s[m] = zero + 1.0
    for lag in range(CHUNK):
        corr_s[lag] = zero

    def step(chunk, _):
        u = [token_row(u_rows, chunk, t) for t in range(CHUNK)]
        d = [token_row(d_rows, chunk, t) for t in range(CHUNK)]
        for lag in range(CHUNK):
            total = corr_s[lag]
            for t in range(CHUNK - lag):
                total = total + d[t + lag] * u[t]
            corr_s[lag] = total
        offset = (chunk * CHUNK).astype(F32)
        for m in range(modes):
            lam = lam_s[m]
            end, endl = u[0], None
            for t in range(1, CHUNK):
                endl = end if endl is None else endl * lam + end
                end = end * lam + u[t]
            head, headl = d[CHUNK - 1], None
            for t in range(CHUNK - 2, -1, -1):
                headl = head if headl is None else headl * lam + head
                head = head * lam + d[t]
            c_ref[0, chunk, m] = end
            b_ref[0, chunk, m] = head
            state, lag_state = state_s[m], lag_s[m]
            res_s[m] = res_s[m] + head * state
            mixl_s[m] = mixl_s[m] + (headl * state + head * lag_state)
            jump = jump_s[m]
            lag_s[m] = lag_state * jump + (state * slope_s[m] + endl)
            state_s[m] = state * jump + end
            power = pow_s[m]
            far = power * head
            head_s[m] = head_s[m] + far
            headl_s[m] = headl_s[m] + power * headl
            headm_s[m] = headm_s[m] + offset * far
            pow_s[m] = power * jump
        return 0

    lax.fori_loop(0, chunks, step, 0)
    def stats_of(m):
        lam = lam_s[m]
        near, nearl = corr_s[CHUNK - 1], None
        for lag in range(CHUNK - 2, -1, -1):
            nearl = near if nearl is None else nearl * lam + near
            near = near * lam + corr_s[lag]
        res = res_s[m]
        return (
            state_s[m],
            lam * lag_s[m],
            head_s[m],
            lam * headl_s[m] + headm_s[m],
            near + lam * res,
            lam * (nearl + (res + lam * mixl_s[m])),
        )

    half = modes // 2
    for m in range(half):
        kept_ref[6, 0, m] = jnp.where(first, rate_ref[0, m], rate_ref[0, m + half])
        for i, (low, high) in enumerate(zip(stats_of(m), stats_of(m + half))):
            kept_ref[i, 0, m] = jnp.where(first, low, high)
            send_ref[i, 0, m] = jnp.where(first, high, low)


def local_kernel(
    k_ref, v_ref, q_ref, g_ref, rate_ref, residue_ref, c_ref, b_ref, after_ref,
    z_ref, w_ref, zeros_ref, u_rows, d_rows, r_rows, lam_s, jump_s, lead_s, state_s, back_s, tap_s,
):
    modes = rate_ref.shape[1]
    chunks = k_ref.shape[0] // CHUNK
    zeros_ref[...] = jnp.zeros((1, LANES), F32)
    to_rows(k_ref, v_ref, u_rows)
    to_rows(g_ref, q_ref, d_rows)
    mode_rows(residue_ref, r_rows)
    zero = jnp.zeros((SUBS, LANES), F32)
    taps = [zero for _ in range(CHUNK)]
    for m in range(modes):
        rate = rate_ref[0, m]
        lam = jnp.exp(-rate)
        square = lam * lam
        fourth = square * square
        lam_s[m] = lam
        jump_s[m] = fourth * fourth
        power = mode_row(r_rows, m) * jnp.sqrt(2.0 * rate)
        lead_s[m] = power * lam
        for lag in range(CHUNK):
            taps[lag] = taps[lag] + power
            power = power * lam
        state_s[m] = zero
        back_s[m] = zero
    for lag in range(CHUNK):
        tap_s[lag] = taps[lag]

    def step(chunk, _):
        mirror = chunks - 1 - chunk
        u = [token_row(u_rows, chunk, t) for t in range(CHUNK)]
        z = [None] * CHUNK
        for lag in range(CHUNK):
            tap = tap_s[lag]
            for t in range(lag, CHUNK):
                term = tap * u[t - lag]
                z[t] = term if z[t] is None else z[t] + term
        d = [token_row(d_rows, mirror, t) for t in range(CHUNK)]
        w = [None] * CHUNK
        for lag in range(CHUNK):
            tap = tap_s[lag]
            for t in range(CHUNK - lag):
                term = tap * d[t + lag]
                w[t] = term if w[t] is None else w[t] + term
        for m in range(modes):
            lam, lead, jump = lam_s[m], lead_s[m], jump_s[m]
            state, back = state_s[m], back_s[m]
            ahead, behind = state * lead, back * lead
            for t in range(CHUNK):
                z[t] = z[t] + ahead
                w[CHUNK - 1 - t] = w[CHUNK - 1 - t] + behind
                if t + 1 < CHUNK:
                    ahead = ahead * lam
                    behind = behind * lam
            state_s[m] = state * jump + c_ref[0, chunk, m]
            back_s[m] = back * jump + b_ref[0, mirror, m]
        for t in range(CHUNK):
            z_ref[0, chunk * CHUNK + t] = z[t]
            w_ref[0, mirror * CHUNK + t] = w[t]
        return 0

    lax.fori_loop(0, chunks, step, 0)


def output_kernel(
    earlier, k_ref, v_ref, q_ref, g_ref, rate_ref, residue_ref, zl_ref, wl_ref, kept_ref, got_ref, after_ref, *refs
):
    mixed_ref, qg_ref, kg_ref, vg_ref, zeros_ref = refs[earlier : earlier + 5]
    z_rows, w_rows, r_rows, lam_s, ahead_s, behind_s = refs[earlier + 5 :]
    modes = rate_ref.shape[1]
    half = modes // 2
    chunks = k_ref.shape[0] // CHUNK
    first = lax.axis_index("ctx") % 2 == 0
    zeros_ref[...] = jnp.zeros((1, LANES), F32)
    mode_rows(residue_ref, r_rows)
    for m in range(modes):
        rate = rate_ref[0, m]
        lam = jnp.exp(-rate)
        lam_s[m] = lam
        lead = mode_row(r_rows, m) * jnp.sqrt(2.0 * rate) * lam
        mine = first if m < half else jnp.logical_not(first)
        ahead_s[m] = lead * jnp.where(mine, kept_ref[0, 0, m % half], got_ref[0, 0, m % half])
        behind_s[m] = lead * jnp.where(mine, kept_ref[1, 0, m % half], got_ref[1, 0, m % half])

    def step(chunk, _):
        mirror = chunks - 1 - chunk
        z = [zl_ref[0, chunk * CHUNK + t] for t in range(CHUNK)]
        w = [wl_ref[0, mirror * CHUNK + t] for t in range(CHUNK)]
        for m in range(modes):
            lam = lam_s[m]
            ahead, behind = ahead_s[m], behind_s[m]
            for t in range(CHUNK):
                z[t] = z[t] + ahead
                ahead = ahead * lam
                w[CHUNK - 1 - t] = w[CHUNK - 1 - t] + behind
                behind = behind * lam
            ahead_s[m] = ahead
            behind_s[m] = behind
        for t in range(CHUNK):
            z_rows[pl.ds(chunk * 64 + t, 8, stride=8), :] = z[t]
            w_rows[pl.ds(mirror * 64 + t, 8, stride=8), :] = w[t]
        return 0

    lax.fori_loop(0, chunks, step, 0)
    for pair in range(chunks // 2):
        window = pl.ds(pair * 16, 16)
        for tile in range(SUBS):
            lanes = pl.ds(tile * LANES, LANES)
            z = jnp.concatenate([z_rows[pl.ds((pair * 2 + part) * 64 + tile * 8, 8), :] for part in range(2)], axis=0)
            w = jnp.concatenate([w_rows[pl.ds((pair * 2 + part) * 64 + tile * 8, 8), :] for part in range(2)], axis=0)
            mixed_ref[window, lanes] = (q_ref[window, lanes].astype(F32) * z).astype(jnp.bfloat16)
            qg_ref[window, lanes] = (g_ref[window, lanes].astype(F32) * z).astype(jnp.bfloat16)
            kg_ref[window, lanes] = (w * v_ref[window, lanes].astype(F32)).astype(jnp.bfloat16)
            vg_ref[window, lanes] = (w * k_ref[window, lanes].astype(F32)).astype(jnp.bfloat16)


def chip_of():
    me = lax.axis_index("ctx")
    return me % 2, me // 2


def joined_in(doc_ref, chip):
    return (doc_ref[0, 2 * chip] == doc_ref[0, 2 * chip + 1]).astype(F32)


def merge_kernel(block, chips, doc_ref, kept_ref, got_ref, *refs):
    outs, part_ref, chip_ref = refs[:chips], refs[chips], refs[chips + 1]
    core, chip = chip_of()
    first = core == 0
    half = kept_ref.shape[1]
    part = half // chips
    joined = joined_in(doc_ref, chip)
    rate = kept_ref[6]
    part_ref[...] = kept_ref[6, pl.ds(pl.multiple_of(chip * part, part), part), :]
    hop = joined * jnp.exp(-block * rate)
    link = joined * jnp.exp(-rate)
    left = [jnp.where(first, kept_ref[i], got_ref[i]) for i in range(6)]
    right = [jnp.where(first, got_ref[i], kept_ref[i]) for i in range(6)]
    chip_ref[0] = right[0] + hop * left[0]
    chip_ref[1] = right[1] + hop * (left[1] + block * left[0])
    chip_ref[2] = left[2] + hop * right[2]
    chip_ref[3] = left[3] + hop * (right[3] + block * right[2])
    chip_ref[4] = left[4] + right[4] + link * (right[2] * left[0])
    chip_ref[5] = left[5] + right[5] + link * ((right[3] + right[2]) * left[0] + right[2] * left[1])
    for away in range(chips):
        start = pl.multiple_of((chip ^ away) * part, part)
        outs[away][...] = chip_ref[:, pl.ds(start, part), :]


def scan_kernel(block, chips, doc_ref, rate_ref, *refs):
    refs = refs[:chips] + refs[chips + 1 :]
    ins, outs, total_ref = refs[:chips], refs[chips : 2 * chips], refs[2 * chips]
    ordered, ends = refs[2 * chips + 1], refs[2 * chips + 2]
    core, chip = chip_of()
    for away in range(chips):
        ordered[chip ^ away] = ins[away][...]
    rate = rate_ref[...]
    lam = jnp.exp(-rate)
    span = 2.0 * block
    hop = jnp.exp(-span * rate)
    zero = jnp.zeros_like(rate)
    state, lag_state, res, grad_lag = zero, zero, zero, zero
    for j in range(chips):
        ends[j, 0] = state
        res = res + (ordered[j, 4] + lam * (ordered[j, 2] * state))
        grad_lag = grad_lag + (
            ordered[j, 5]
            + lam * ((ordered[j, 3] + ordered[j, 2]) * state + ordered[j, 2] * lag_state)
        )
        if j + 1 < chips:
            through = joined_in(doc_ref, j) * hop
            keep = (doc_ref[0, 2 * j + 1] == doc_ref[0, 2 * j + 2]).astype(F32)
            lag_state = keep * (ordered[j, 1] + through * (lag_state + span * state))
            state = keep * (ordered[j, 0] + through * state)
    back = zero
    for j in range(chips - 1, -1, -1):
        ends[j, 1] = back
        if j > 0:
            through = joined_in(doc_ref, j) * hop
            keep = (doc_ref[0, 2 * j - 1] == doc_ref[0, 2 * j]).astype(F32)
            back = keep * (ordered[j, 2] + through * back)
    for away in range(chips):
        outs[away][...] = ends[chip ^ away]
    total_ref[0] = res
    total_ref[1] = grad_lag


def expand_kernel(block, chips, doc_ref, kept_ref, got_ref, *refs):
    ins, mine_ref, send_ref, whole = refs[:chips], refs[chips], refs[chips + 1], refs[chips + 2]
    core, chip = chip_of()
    first = core == 0
    joined = joined_in(doc_ref, chip)
    part = ins[0].shape[1]
    for away in range(chips):
        start = pl.multiple_of((chip ^ away) * part, part)
        whole[:, pl.ds(start, part), :] = ins[away][...]
    hop = joined * jnp.exp(-block * kept_ref[6])
    end_left = jnp.where(first, kept_ref[0], got_ref[0])
    head_right = jnp.where(first, got_ref[2], kept_ref[2])
    state, back = whole[0], whole[1]
    state_right = joined * end_left + hop * state
    back_left = joined * head_right + hop * back
    mine_ref[0] = jnp.where(first, state, state_right)
    mine_ref[1] = jnp.where(first, back_left, back)
    send_ref[0] = jnp.where(first, state_right, state)
    send_ref[1] = jnp.where(first, back, back_left)


def gather_kernel(chips, *refs):
    ins, out_ref = refs[:chips], refs[chips + 1]
    core, chip = chip_of()
    part = ins[0].shape[1]
    for away in range(chips):
        start = pl.multiple_of((chip ^ away) * part, part)
        out_ref[:, pl.ds(start, part), :] = ins[away][...]


def final_kernel(scale, rate_ref, residue_ref, kept_ref, got_ref, res_ref, grad_ref, sums, res_rows, grad_rows):
    core, chip = chip_of()
    half = kept_ref.shape[1]
    sums[:, pl.ds(pl.multiple_of(core * half, half), half), :] = kept_ref[...]
    sums[:, pl.ds(pl.multiple_of((1 - core) * half, half), half), :] = got_ref[...]
    modes, channels = residue_ref.shape
    halves = modes // 2
    for group in range(channels // GROUP):
        for m in range(modes):
            window = pl.ds((m // halves) * half + (group * halves + m % halves) * SUBS, SUBS)
            rate = rate_ref[group, m]
            root = jnp.sqrt(2.0 * rate) * scale
            grad_res, grad_lag = sums[0, window, :], sums[1, window, :]
            target = pl.ds((m // 8) * 64 + m % 8, 8, stride=8)
            res_rows[target, :] = root * grad_res
            grad_rows[target, :] = root * (0.5 * grad_res - rate * grad_lag)
        for eight in range(modes // 8):
            for tile in range(SUBS):
                place = (pl.ds(eight * 8, 8), pl.ds(group * GROUP + tile * LANES, LANES))
                rows = pl.ds(eight * 64 + tile * 8, 8)
                res_ref[place] = res_rows[rows, :]
                grad_ref[place] = residue_ref[place] * grad_rows[rows, :]


def whole(array):
    rank = len(array.shape)
    return pl.BlockSpec(array.shape, lambda i: (0,) * rank)


def unread():
    return pl.BlockSpec(memory_space=pl.ANY)


def small_call(kernel, name, ins, outs, scratch, after=()):
    return pl.pallas_call(
        kernel,
        grid=(1,),
        in_specs=[scalar_spec() if x.dtype == jnp.int32 else whole(x) for x in ins] + [unread() for _ in after],
        out_specs=[whole(x) for x in outs],
        out_shape=outs,
        scratch_shapes=scratch,
        compiler_params=params(),
        name=name,
    )(*ins, *after)


def hbm(x):
    return pltpu.with_memory_space_constraint(x, pltpu.HBM)


def vmem(x):
    return pltpu.with_memory_space_constraint(x, pltpu.VMEM)


def f32(*shape):
    return jax.ShapeDtypeStruct(shape, F32)


def scalar_spec():
    return pl.BlockSpec(memory_space=pltpu.SMEM)


def params(mib=16):
    return pltpu.CompilerParams(vmem_limit_bytes=mib * 1024 * 1024)


def body(q_proj, k_proj, v_proj, out_grad, residue, pole_decay, group_doc):
    block, channels = q_proj.shape[1], q_proj.shape[2]
    modes = residue.shape[0]
    n_ctx, n_dp = lax.axis_size("ctx"), lax.axis_size("dp")
    row_len = block * n_ctx
    total_tokens = row_len * n_dp
    chips = n_ctx // 2
    groups = channels // GROUP
    chunks = block // CHUNK
    rows = modes * channels // LANES
    half = rows // 2
    part = half // chips
    halves = modes // 2

    tokens = [x.reshape(block, channels) for x in (k_proj, v_proj, q_proj, out_grad)]
    k_in, v_in, q_in, g_in = (hbm(x) for x in tokens)
    row_scratch = pltpu.VMEM((block * SUBS, LANES), F32)
    mode_scratch = pltpu.VMEM((modes, SUBS, LANES), F32)
    flat_scratch = pltpu.VMEM((modes * SUBS, LANES), F32)
    tap_scratch = pltpu.VMEM((CHUNK, SUBS, LANES), F32)

    def specs(at):
        return (
            pl.BlockSpec((block, GROUP), lambda i: (0, at(i))),
            pl.BlockSpec((1, modes, SUBS, LANES), lambda i: (at(i), 0, 0, 0)),
            pl.BlockSpec((modes, GROUP), lambda i: (0, at(i))),
            pl.BlockSpec((1, chunks, modes, SUBS, LANES), lambda i: (at(i), 0, 0, 0, 0)),
            lambda count: pl.BlockSpec((count, 1, halves, SUBS, LANES), lambda i: (0, at(i), 0, 0, 0)),
        )

    wide, slim, natural, chunked, halved = specs(lambda i: i)
    ends, heads, rate, kept, send = pl.pallas_call(
        partial(stats_kernel, float(row_len)),
        grid=(groups,),
        in_specs=[wide] * 4 + [natural],
        out_specs=[chunked, chunked, slim, halved(7), halved(6)],
        out_shape=[
            pltpu.VMEM((groups, chunks, modes, SUBS, LANES), F32),
            pltpu.VMEM((groups, chunks, modes, SUBS, LANES), F32),
            pltpu.VMEM((groups, modes, SUBS, LANES), F32),
            pltpu.VMEM((7, groups, halves, SUBS, LANES), F32),
            pltpu.VMEM((6, groups, halves, SUBS, LANES), F32),
        ],
        scratch_shapes=[row_scratch] * 2 + [flat_scratch] + [mode_scratch] * 11 + [tap_scratch],
        compiler_params=params(BIG),
        name="block_stats",
    )(k_in, v_in, q_in, g_in, hbm(pole_decay))

    kept = kept.reshape(7, half, LANES)
    send = send.reshape(6, half, LANES)

    def swap_core(x):
        return lax.ppermute(x, "ctx", [(i, i ^ 1) for i in range(n_ctx)])

    def swap_chips(xs):
        return [xs[0]] + [
            lax.ppermute(xs[away], "ctx", [(i, i ^ (2 * away)) for i in range(n_ctx)]) for away in range(1, chips)
        ]

    got = swap_core(send)
    *pieces, rate_part = small_call(
        partial(merge_kernel, float(block), chips),
        "chip_stats",
        [group_doc, kept, got],
        [f32(6, part, LANES)] * chips + [f32(part, LANES)],
        [pltpu.VMEM((6, half, LANES), F32)],
    )
    columns = pl.BlockSpec((1, block, SUBS, LANES), lambda i: (i, 0, 0, 0))
    z_local, w_local, zeros = pl.pallas_call(
        local_kernel,
        grid=(groups,),
        in_specs=[wide] * 4 + [slim, natural] + [chunked] * 2 + [pl.BlockSpec(memory_space=pl.ANY)],
        out_specs=[columns] * 2 + [pl.BlockSpec((1, LANES), lambda i: (0, 0))],
        out_shape=[pltpu.VMEM((groups, block, SUBS, LANES), F32)] * 2 + [pltpu.VMEM((1, LANES), F32)],
        scratch_shapes=[row_scratch] * 2 + [flat_scratch] + [mode_scratch] * 5 + [tap_scratch],
        compiler_params=params(BIG),
        cost_estimate=pl.CostEstimate(flops=10_000_000_000, bytes_accessed=20_000_000, transcendentals=0),
        name="local_outputs",
    )(k_in, v_in, q_in, g_in, vmem(rate), hbm(residue), vmem(ends), vmem(heads), rate_part)
    scanned = small_call(
        partial(scan_kernel, float(block), chips),
        "row_scan",
        [group_doc, rate_part, *swap_chips(pieces)],
        [f32(2, part, LANES)] * (chips + 1),
        [pltpu.VMEM((chips, 6, part, LANES), F32), pltpu.VMEM((chips, 2, part, LANES), F32)],
        after=[zeros],
    )
    total = scanned[chips]
    for other in [lax.ppermute(total, "dp", [(i, i ^ away) for i in range(n_dp)]) for away in range(1, n_dp)]:
        total = total + other
    mine, give = small_call(
        partial(expand_kernel, float(block), chips),
        "block_edges",
        [group_doc, kept, got, *swap_chips(scanned[:chips])],
        [f32(2, half, LANES)] * 2,
        [pltpu.VMEM((2, half, LANES), F32)],
    )
    theirs = swap_core(give)

    edges = [x.reshape(2, groups, halves, SUBS, LANES) for x in (mine, theirs)]

    held = [vmem(x) for x in (*tokens, rate, residue)]

    def outputs(first, count, after, outs):
        wide, slim, natural, chunked, halved = specs(lambda i: i + first)
        columns = pl.BlockSpec((1, block, SUBS, LANES), lambda i: (i + first, 0, 0, 0))
        result = pl.pallas_call(
            partial(output_kernel, len(outs)),
            grid=(count,),
            in_specs=[wide] * 4 + [slim, natural] + [columns] * 2 + [halved(2)] * 2
            + [pl.BlockSpec(memory_space=pl.ANY)] * (1 + len(outs)),
            out_specs=[wide] * 4 + [pl.BlockSpec((1, LANES), lambda i: (0, 0))],
            out_shape=[pltpu.HBM((block, channels), jnp.bfloat16)] * 4 + [pltpu.VMEM((1, LANES), F32)],
            input_output_aliases={11 + i: i for i in range(len(outs))},
            scratch_shapes=[row_scratch] * 2 + [flat_scratch] + [mode_scratch] * 3,
            compiler_params=params(BIG),
            cost_estimate=pl.CostEstimate(
                flops=100_000_000 * count, bytes_accessed=500_000 * count, transcendentals=0
            ),
            name="outputs",
        )(*held, vmem(z_local), vmem(w_local), *edges, after, *outs)
        return result[:4], result[4]

    sums = swap_chips([total] * chips)
    cut = (3 * groups + 3) // 4
    outs, zeros = outputs(0, cut, total, [])
    (gathered,) = small_call(
        partial(gather_kernel, chips), "gather_sums", sums, [f32(2, half, LANES)], [], after=[zeros]
    )
    if cut < groups:
        outs, _ = outputs(cut, groups - cut, gathered, outs)
    residue_grad, pole_grad = small_call(
        partial(final_kernel, 1.0 / math.sqrt(total_tokens)),
        "parameter_grads",
        [rate, residue, gathered, swap_core(gathered)],
        [f32(modes, channels)] * 2,
        [pltpu.VMEM((2, rows, LANES), F32)] + [flat_scratch] * 2,
    )
    return (*(x[None] for x in outs), residue_grad, pole_grad)


def solution(mesh):
    tokens = P("dp", "ctx", None)
    return jax.shard_map(
        body,
        mesh=mesh,
        in_specs=(tokens, tokens, tokens, tokens, P(), P(), P("dp", None)),
        out_specs=(tokens, tokens, tokens, tokens, P(), P()),
        check_vma=False,
    )
```

```python
from functools import partial
import math

import jax
import jax.numpy as jnp
from jax import lax
from jax.experimental import pallas as pl
from jax.experimental.pallas import tpu as pltpu
from jax.sharding import PartitionSpec as P

F32 = jnp.float32
LANES = 128
SUBS = 8
GROUP = LANES * SUBS
CHUNK = 8
BIG = 32


def to_rows(left_ref, right_ref, rows_ref):
    tokens = left_ref.shape[0]
    for pair in range(tokens // 16):
        window = pl.ds(pair * 16, 16)
        for tile in range(SUBS):
            lanes = pl.ds(tile * LANES, LANES)
            product = left_ref[window, lanes].astype(F32) * right_ref[window, lanes].astype(F32)
            for part in range(2):
                start = (pair * 2 + part) * 64 + tile * 8
                rows_ref[pl.ds(start, 8), :] = product[part * 8 : part * 8 + 8]


def token_row(rows_ref, chunk, token):
    return rows_ref[pl.ds(chunk * 64 + token, 8, stride=8), :]


def mode_rows(natural_ref, rows_ref):
    for eight in range(natural_ref.shape[0] // 8):
        for tile in range(SUBS):
            rows_ref[pl.ds(eight * 64 + tile * 8, 8), :] = natural_ref[
                pl.ds(eight * 8, 8), pl.ds(tile * LANES, LANES)
            ]


def mode_row(rows_ref, mode):
    return rows_ref[pl.ds((mode // 8) * 64 + mode % 8, 8, stride=8), :]


def stats_kernel(
    row_len, k_ref, v_ref, q_ref, g_ref, pole_ref, c_ref, b_ref, rate_ref, kept_ref, send_ref,
    u_rows, d_rows, p_rows, lam_s, jump_s, slope_s, state_s, lag_s, res_s, mixl_s, head_s, headl_s, headm_s, pow_s,
    corr_s,
):
    modes = pole_ref.shape[0]
    chunks = k_ref.shape[0] // CHUNK
    first = lax.axis_index("ctx") % 2 == 0
    to_rows(k_ref, v_ref, u_rows)
    to_rows(g_ref, q_ref, d_rows)
    mode_rows(pole_ref, p_rows)
    zero = jnp.zeros((SUBS, LANES), F32)
    for m in range(modes):
        rate = mode_row(p_rows, m) / row_len
        rate_ref[0, m] = rate
        lam = jnp.exp(-rate)
        square = lam * lam
        fourth = square * square
        cube = square * lam
        for j, power in enumerate((lam, square, cube, fourth, fourth * lam, fourth * square, fourth * cube)):
            lam_s[m, j] = power
        jump_s[m] = fourth * fourth
        slope_s[m] = CHUNK * (fourth * fourth)
        for ref in (state_s, lag_s, res_s, mixl_s, head_s, headl_s, headm_s):
            ref[m] = zero
        pow_s[m] = zero + 1.0
    for lag in range(CHUNK):
        corr_s[lag] = zero

    def step(chunk, _):
        u = [token_row(u_rows, chunk, t) for t in range(CHUNK)]
        d = [token_row(d_rows, chunk, t) for t in range(CHUNK)]
        for lag in range(CHUNK):
            total = corr_s[lag]
            for t in range(CHUNK - lag):
                total = total + d[t + lag] * u[t]
            corr_s[lag] = total
        offset = (chunk * CHUNK).astype(F32)
        for m in range(modes):
            power = [lam_s[m, j] for j in range(CHUNK - 1)]
            end, head = power[-1] * u[0], power[-1] * d[-1]
            endl, headl = end, head
            for j in range(CHUNK - 2, 0, -1):
                end = end + power[j - 1] * u[CHUNK - 1 - j]
                endl = endl + end
                head = head + power[j - 1] * d[j]
                headl = headl + head
            end, head = end + u[-1], head + d[0]
            c_ref[0, chunk, m] = end
            b_ref[0, chunk, m] = head
            state, lag_state = state_s[m], lag_s[m]
            res_s[m] = res_s[m] + head * state
            mixl_s[m] = mixl_s[m] + (headl * state + head * lag_state)
            jump = jump_s[m]
            lag_s[m] = lag_state * jump + (state * slope_s[m] + endl)
            state_s[m] = state * jump + end
            decay = pow_s[m]
            far = decay * head
            head_s[m] = head_s[m] + far
            headl_s[m] = headl_s[m] + decay * headl
            headm_s[m] = headm_s[m] + offset * far
            pow_s[m] = decay * jump
        return 0

    lax.fori_loop(0, chunks, step, 0)
    def stats_of(m):
        lam = lam_s[m, 0]
        near, nearl = corr_s[CHUNK - 1], None
        for lag in range(CHUNK - 2, -1, -1):
            nearl = near if nearl is None else nearl * lam + near
            near = near * lam + corr_s[lag]
        res = res_s[m]
        return (
            state_s[m],
            lag_s[m],
            head_s[m],
            headl_s[m] + headm_s[m],
            near + lam * res,
            lam * (nearl + (res + mixl_s[m])),
        )

    half = modes // 2
    for m in range(half):
        kept_ref[6, 0, m] = jnp.where(first, rate_ref[0, m], rate_ref[0, m + half])
        for i, (low, high) in enumerate(zip(stats_of(m), stats_of(m + half))):
            kept_ref[i, 0, m] = jnp.where(first, low, high)
            send_ref[i, 0, m] = jnp.where(first, high, low)


def local_kernel(
    k_ref, v_ref, q_ref, g_ref, rate_ref, residue_ref, c_ref, b_ref, after_ref,
    z_ref, w_ref, zeros_ref, u_rows, d_rows, r_rows, lam_s, jump_s, lead_s, state_s, back_s, tap_s,
):
    modes = rate_ref.shape[1]
    chunks = k_ref.shape[0] // CHUNK
    zeros_ref[...] = jnp.zeros((1, LANES), F32)
    to_rows(k_ref, v_ref, u_rows)
    to_rows(g_ref, q_ref, d_rows)
    mode_rows(residue_ref, r_rows)
    zero = jnp.zeros((SUBS, LANES), F32)
    taps = [zero for _ in range(CHUNK)]
    for m in range(modes):
        rate = rate_ref[0, m]
        lam = jnp.exp(-rate)
        square = lam * lam
        fourth = square * square
        lam_s[m] = lam
        jump_s[m] = fourth * fourth
        power = mode_row(r_rows, m) * jnp.sqrt(2.0 * rate)
        lead_s[m] = power * lam
        for lag in range(CHUNK):
            taps[lag] = taps[lag] + power
            power = power * lam
        state_s[m] = zero
        back_s[m] = zero
    for lag in range(CHUNK):
        tap_s[lag] = taps[lag]

    def step(chunk, _):
        mirror = chunks - 1 - chunk
        u = [token_row(u_rows, chunk, t) for t in range(CHUNK)]
        z = [None] * CHUNK
        for lag in range(CHUNK):
            tap = tap_s[lag]
            for t in range(lag, CHUNK):
                term = tap * u[t - lag]
                z[t] = term if z[t] is None else z[t] + term
        d = [token_row(d_rows, mirror, t) for t in range(CHUNK)]
        w = [None] * CHUNK
        for lag in range(CHUNK):
            tap = tap_s[lag]
            for t in range(CHUNK - lag):
                term = tap * d[t + lag]
                w[t] = term if w[t] is None else w[t] + term
        for m in range(modes):
            lam, lead, jump = lam_s[m], lead_s[m], jump_s[m]
            state, back = state_s[m], back_s[m]
            ahead, behind = state * lead, back * lead
            for t in range(CHUNK):
                z[t] = z[t] + ahead
                w[CHUNK - 1 - t] = w[CHUNK - 1 - t] + behind
                if t + 1 < CHUNK:
                    ahead = ahead * lam
                    behind = behind * lam
            state_s[m] = state * jump + c_ref[0, chunk, m]
            back_s[m] = back * jump + b_ref[0, mirror, m]
        for t in range(CHUNK):
            z_ref[0, chunk * CHUNK + t] = z[t]
            w_ref[0, mirror * CHUNK + t] = w[t]
        return 0

    lax.fori_loop(0, chunks, step, 0)


def output_kernel(
    earlier, k_ref, v_ref, q_ref, g_ref, rate_ref, residue_ref, zl_ref, wl_ref, kept_ref, got_ref, after_ref, *refs
):
    mixed_ref, qg_ref, kg_ref, vg_ref, zeros_ref = refs[earlier : earlier + 5]
    z_rows, w_rows, r_rows, lam_s, ahead_s, behind_s = refs[earlier + 5 :]
    modes = rate_ref.shape[1]
    half = modes // 2
    chunks = k_ref.shape[0] // CHUNK
    first = lax.axis_index("ctx") % 2 == 0
    zeros_ref[...] = jnp.zeros((1, LANES), F32)
    mode_rows(residue_ref, r_rows)
    for m in range(modes):
        rate = rate_ref[0, m]
        lam = jnp.exp(-rate)
        lam_s[m] = lam
        lead = mode_row(r_rows, m) * jnp.sqrt(2.0 * rate) * lam
        mine = first if m < half else jnp.logical_not(first)
        ahead_s[m] = lead * jnp.where(mine, kept_ref[0, 0, m % half], got_ref[0, 0, m % half])
        behind_s[m] = lead * jnp.where(mine, kept_ref[1, 0, m % half], got_ref[1, 0, m % half])

    def step(chunk, _):
        mirror = chunks - 1 - chunk
        z = [zl_ref[0, chunk * CHUNK + t] for t in range(CHUNK)]
        w = [wl_ref[0, mirror * CHUNK + t] for t in range(CHUNK)]
        for m in range(modes):
            lam = lam_s[m]
            ahead, behind = ahead_s[m], behind_s[m]
            for t in range(CHUNK):
                z[t] = z[t] + ahead
                ahead = ahead * lam
                w[CHUNK - 1 - t] = w[CHUNK - 1 - t] + behind
                behind = behind * lam
            ahead_s[m] = ahead
            behind_s[m] = behind
        for t in range(CHUNK):
            z_rows[pl.ds(chunk * 64 + t, 8, stride=8), :] = z[t]
            w_rows[pl.ds(mirror * 64 + t, 8, stride=8), :] = w[t]
        return 0

    lax.fori_loop(0, chunks, step, 0)
    for pair in range(chunks // 2):
        window = pl.ds(pair * 16, 16)
        for tile in range(SUBS):
            lanes = pl.ds(tile * LANES, LANES)
            z = jnp.concatenate([z_rows[pl.ds((pair * 2 + part) * 64 + tile * 8, 8), :] for part in range(2)], axis=0)
            w = jnp.concatenate([w_rows[pl.ds((pair * 2 + part) * 64 + tile * 8, 8), :] for part in range(2)], axis=0)
            mixed_ref[window, lanes] = (q_ref[window, lanes].astype(F32) * z).astype(jnp.bfloat16)
            qg_ref[window, lanes] = (g_ref[window, lanes].astype(F32) * z).astype(jnp.bfloat16)
            kg_ref[window, lanes] = (w * v_ref[window, lanes].astype(F32)).astype(jnp.bfloat16)
            vg_ref[window, lanes] = (w * k_ref[window, lanes].astype(F32)).astype(jnp.bfloat16)


def chip_of():
    me = lax.axis_index("ctx")
    return me % 2, me // 2


def joined_in(doc_ref, chip):
    return (doc_ref[0, 2 * chip] == doc_ref[0, 2 * chip + 1]).astype(F32)


def merge_kernel(block, chips, doc_ref, kept_ref, got_ref, *refs):
    outs, part_ref, chip_ref = refs[:chips], refs[chips], refs[chips + 1]
    core, chip = chip_of()
    first = core == 0
    half = kept_ref.shape[1]
    part = half // chips
    joined = joined_in(doc_ref, chip)
    rate = kept_ref[6]
    part_ref[...] = kept_ref[6, pl.ds(pl.multiple_of(chip * part, part), part), :]
    hop = joined * jnp.exp(-block * rate)
    link = joined * jnp.exp(-rate)
    left = [jnp.where(first, kept_ref[i], got_ref[i]) for i in range(6)]
    right = [jnp.where(first, got_ref[i], kept_ref[i]) for i in range(6)]
    chip_ref[0] = right[0] + hop * left[0]
    chip_ref[1] = right[1] + hop * (left[1] + block * left[0])
    chip_ref[2] = left[2] + hop * right[2]
    chip_ref[3] = left[3] + hop * (right[3] + block * right[2])
    chip_ref[4] = left[4] + right[4] + link * (right[2] * left[0])
    chip_ref[5] = left[5] + right[5] + link * ((right[3] + right[2]) * left[0] + right[2] * left[1])
    for away in range(chips):
        start = pl.multiple_of((chip ^ away) * part, part)
        outs[away][...] = chip_ref[:, pl.ds(start, part), :]


def scan_kernel(block, chips, doc_ref, rate_ref, *refs):
    refs = refs[:chips] + refs[chips + 1 :]
    ins, outs, total_ref = refs[:chips], refs[chips : 2 * chips], refs[2 * chips]
    ordered, ends = refs[2 * chips + 1], refs[2 * chips + 2]
    core, chip = chip_of()
    for away in range(chips):
        ordered[chip ^ away] = ins[away][...]
    rate = rate_ref[...]
    lam = jnp.exp(-rate)
    span = 2.0 * block
    hop = jnp.exp(-span * rate)
    zero = jnp.zeros_like(rate)
    state, lag_state, res, grad_lag = zero, zero, zero, zero
    for j in range(chips):
        ends[j, 0] = state
        res = res + (ordered[j, 4] + lam * (ordered[j, 2] * state))
        grad_lag = grad_lag + (
            ordered[j, 5]
            + lam * ((ordered[j, 3] + ordered[j, 2]) * state + ordered[j, 2] * lag_state)
        )
        if j + 1 < chips:
            through = joined_in(doc_ref, j) * hop
            keep = (doc_ref[0, 2 * j + 1] == doc_ref[0, 2 * j + 2]).astype(F32)
            lag_state = keep * (ordered[j, 1] + through * (lag_state + span * state))
            state = keep * (ordered[j, 0] + through * state)
    back = zero
    for j in range(chips - 1, -1, -1):
        ends[j, 1] = back
        if j > 0:
            through = joined_in(doc_ref, j) * hop
            keep = (doc_ref[0, 2 * j - 1] == doc_ref[0, 2 * j]).astype(F32)
            back = keep * (ordered[j, 2] + through * back)
    for away in range(chips):
        outs[away][...] = ends[chip ^ away]
    total_ref[0] = res
    total_ref[1] = grad_lag


def expand_kernel(block, chips, doc_ref, kept_ref, got_ref, *refs):
    ins, mine_ref, send_ref, whole = refs[:chips], refs[chips], refs[chips + 1], refs[chips + 2]
    core, chip = chip_of()
    first = core == 0
    joined = joined_in(doc_ref, chip)
    part = ins[0].shape[1]
    for away in range(chips):
        start = pl.multiple_of((chip ^ away) * part, part)
        whole[:, pl.ds(start, part), :] = ins[away][...]
    hop = joined * jnp.exp(-block * kept_ref[6])
    end_left = jnp.where(first, kept_ref[0], got_ref[0])
    head_right = jnp.where(first, got_ref[2], kept_ref[2])
    state, back = whole[0], whole[1]
    state_right = joined * end_left + hop * state
    back_left = joined * head_right + hop * back
    mine_ref[0] = jnp.where(first, state, state_right)
    mine_ref[1] = jnp.where(first, back_left, back)
    send_ref[0] = jnp.where(first, state_right, state)
    send_ref[1] = jnp.where(first, back, back_left)


def gather_kernel(chips, *refs):
    ins, out_ref = refs[:chips], refs[chips + 1]
    core, chip = chip_of()
    part = ins[0].shape[1]
    for away in range(chips):
        start = pl.multiple_of((chip ^ away) * part, part)
        out_ref[:, pl.ds(start, part), :] = ins[away][...]


def final_kernel(scale, rate_ref, residue_ref, kept_ref, got_ref, res_ref, grad_ref, sums, res_rows, grad_rows):
    core, chip = chip_of()
    half = kept_ref.shape[1]
    sums[:, pl.ds(pl.multiple_of(core * half, half), half), :] = kept_ref[...]
    sums[:, pl.ds(pl.multiple_of((1 - core) * half, half), half), :] = got_ref[...]
    modes, channels = residue_ref.shape
    halves = modes // 2
    for group in range(channels // GROUP):
        for m in range(modes):
            window = pl.ds((m // halves) * half + (group * halves + m % halves) * SUBS, SUBS)
            rate = rate_ref[group, m]
            root = jnp.sqrt(2.0 * rate) * scale
            grad_res, grad_lag = sums[0, window, :], sums[1, window, :]
            target = pl.ds((m // 8) * 64 + m % 8, 8, stride=8)
            res_rows[target, :] = root * grad_res
            grad_rows[target, :] = root * (0.5 * grad_res - rate * grad_lag)
        for eight in range(modes // 8):
            for tile in range(SUBS):
                place = (pl.ds(eight * 8, 8), pl.ds(group * GROUP + tile * LANES, LANES))
                rows = pl.ds(eight * 64 + tile * 8, 8)
                res_ref[place] = res_rows[rows, :]
                grad_ref[place] = residue_ref[place] * grad_rows[rows, :]


def whole(array):
    rank = len(array.shape)
    return pl.BlockSpec(array.shape, lambda i: (0,) * rank)


def unread():
    return pl.BlockSpec(memory_space=pl.ANY)


def small_call(kernel, name, ins, outs, scratch, after=()):
    return pl.pallas_call(
        kernel,
        grid=(1,),
        in_specs=[scalar_spec() if x.dtype == jnp.int32 else whole(x) for x in ins] + [unread() for _ in after],
        out_specs=[whole(x) for x in outs],
        out_shape=outs,
        scratch_shapes=scratch,
        compiler_params=params(),
        name=name,
    )(*ins, *after)


def hbm(x):
    return pltpu.with_memory_space_constraint(x, pltpu.HBM)


def vmem(x):
    return pltpu.with_memory_space_constraint(x, pltpu.VMEM)


def f32(*shape):
    return jax.ShapeDtypeStruct(shape, F32)


def scalar_spec():
    return pl.BlockSpec(memory_space=pltpu.SMEM)


def params(mib=16):
    return pltpu.CompilerParams(vmem_limit_bytes=mib * 1024 * 1024)


def body(q_proj, k_proj, v_proj, out_grad, residue, pole_decay, group_doc):
    block, channels = q_proj.shape[1], q_proj.shape[2]
    modes = residue.shape[0]
    n_ctx, n_dp = lax.axis_size("ctx"), lax.axis_size("dp")
    row_len = block * n_ctx
    total_tokens = row_len * n_dp
    chips = n_ctx // 2
    groups = channels // GROUP
    chunks = block // CHUNK
    rows = modes * channels // LANES
    half = rows // 2
    part = half // chips
    halves = modes // 2

    tokens = [x.reshape(block, channels) for x in (k_proj, v_proj, q_proj, out_grad)]
    k_in, v_in, q_in, g_in = (hbm(x) for x in tokens)
    row_scratch = pltpu.VMEM((block * SUBS, LANES), F32)
    mode_scratch = pltpu.VMEM((modes, SUBS, LANES), F32)
    flat_scratch = pltpu.VMEM((modes * SUBS, LANES), F32)
    tap_scratch = pltpu.VMEM((CHUNK, SUBS, LANES), F32)

    def specs(at):
        return (
            pl.BlockSpec((block, GROUP), lambda i: (0, at(i))),
            pl.BlockSpec((1, modes, SUBS, LANES), lambda i: (at(i), 0, 0, 0)),
            pl.BlockSpec((modes, GROUP), lambda i: (0, at(i))),
            pl.BlockSpec((1, chunks, modes, SUBS, LANES), lambda i: (at(i), 0, 0, 0, 0)),
            lambda count: pl.BlockSpec((count, 1, halves, SUBS, LANES), lambda i: (0, at(i), 0, 0, 0)),
        )

    wide, slim, natural, chunked, halved = specs(lambda i: i)
    ends, heads, rate, kept, send = pl.pallas_call(
        partial(stats_kernel, float(row_len)),
        grid=(groups,),
        in_specs=[wide] * 4 + [natural],
        out_specs=[chunked, chunked, slim, halved(7), halved(6)],
        out_shape=[
            pltpu.VMEM((groups, chunks, modes, SUBS, LANES), F32),
            pltpu.VMEM((groups, chunks, modes, SUBS, LANES), F32),
            pltpu.VMEM((groups, modes, SUBS, LANES), F32),
            pltpu.VMEM((7, groups, halves, SUBS, LANES), F32),
            pltpu.VMEM((6, groups, halves, SUBS, LANES), F32),
        ],
        scratch_shapes=[row_scratch] * 2 + [flat_scratch, pltpu.VMEM((modes, CHUNK - 1, SUBS, LANES), F32)]
        + [mode_scratch] * 10 + [tap_scratch],
        compiler_params=params(BIG),
        name="block_stats",
    )(k_in, v_in, q_in, g_in, hbm(pole_decay))

    kept = kept.reshape(7, half, LANES)
    send = send.reshape(6, half, LANES)

    def swap_core(x):
        return lax.ppermute(x, "ctx", [(i, i ^ 1) for i in range(n_ctx)])

    def swap_chips(xs):
        return [xs[0]] + [
            lax.ppermute(xs[away], "ctx", [(i, i ^ (2 * away)) for i in range(n_ctx)]) for away in range(1, chips)
        ]

    got = swap_core(send)
    *pieces, rate_part = small_call(
        partial(merge_kernel, float(block), chips),
        "chip_stats",
        [group_doc, kept, got],
        [f32(6, part, LANES)] * chips + [f32(part, LANES)],
        [pltpu.VMEM((6, half, LANES), F32)],
    )
    columns = pl.BlockSpec((1, block, SUBS, LANES), lambda i: (i, 0, 0, 0))
    z_local, w_local, zeros = pl.pallas_call(
        local_kernel,
        grid=(groups,),
        in_specs=[wide] * 4 + [slim, natural] + [chunked] * 2 + [pl.BlockSpec(memory_space=pl.ANY)],
        out_specs=[columns] * 2 + [pl.BlockSpec((1, LANES), lambda i: (0, 0))],
        out_shape=[pltpu.VMEM((groups, block, SUBS, LANES), F32)] * 2 + [pltpu.VMEM((1, LANES), F32)],
        scratch_shapes=[row_scratch] * 2 + [flat_scratch] + [mode_scratch] * 5 + [tap_scratch],
        compiler_params=params(BIG),
        cost_estimate=pl.CostEstimate(flops=10_000_000_000, bytes_accessed=20_000_000, transcendentals=0),
        name="local_outputs",
    )(k_in, v_in, q_in, g_in, vmem(rate), hbm(residue), vmem(ends), vmem(heads), rate_part)
    scanned = small_call(
        partial(scan_kernel, float(block), chips),
        "row_scan",
        [group_doc, rate_part, *swap_chips(pieces)],
        [f32(2, part, LANES)] * (chips + 1),
        [pltpu.VMEM((chips, 6, part, LANES), F32), pltpu.VMEM((chips, 2, part, LANES), F32)],
        after=[zeros],
    )
    total = scanned[chips]
    for other in [lax.ppermute(total, "dp", [(i, i ^ away) for i in range(n_dp)]) for away in range(1, n_dp)]:
        total = total + other
    mine, give = small_call(
        partial(expand_kernel, float(block), chips),
        "block_edges",
        [group_doc, kept, got, *swap_chips(scanned[:chips])],
        [f32(2, half, LANES)] * 2,
        [pltpu.VMEM((2, half, LANES), F32)],
    )
    theirs = swap_core(give)

    edges = [x.reshape(2, groups, halves, SUBS, LANES) for x in (mine, theirs)]

    held = [vmem(x) for x in (*tokens, rate, residue)]

    def outputs(first, count, after, outs):
        wide, slim, natural, chunked, halved = specs(lambda i: i + first)
        columns = pl.BlockSpec((1, block, SUBS, LANES), lambda i: (i + first, 0, 0, 0))
        result = pl.pallas_call(
            partial(output_kernel, len(outs)),
            grid=(count,),
            in_specs=[wide] * 4 + [slim, natural] + [columns] * 2 + [halved(2)] * 2
            + [pl.BlockSpec(memory_space=pl.ANY)] * (1 + len(outs)),
            out_specs=[wide] * 4 + [pl.BlockSpec((1, LANES), lambda i: (0, 0))],
            out_shape=[pltpu.HBM((block, channels), jnp.bfloat16)] * 4 + [pltpu.VMEM((1, LANES), F32)],
            input_output_aliases={11 + i: i for i in range(len(outs))},
            scratch_shapes=[row_scratch] * 2 + [flat_scratch] + [mode_scratch] * 3,
            compiler_params=params(BIG),
            cost_estimate=pl.CostEstimate(
                flops=100_000_000 * count, bytes_accessed=500_000 * count, transcendentals=0
            ),
            name="outputs",
        )(*held, vmem(z_local), vmem(w_local), *edges, after, *outs)
        return result[:4], result[4]

    sums = swap_chips([total] * chips)
    cut = (3 * groups + 3) // 4
    outs, zeros = outputs(0, cut, total, [])
    (gathered,) = small_call(
        partial(gather_kernel, chips), "gather_sums", sums, [f32(2, half, LANES)], [], after=[zeros]
    )
    if cut < groups:
        outs, _ = outputs(cut, groups - cut, gathered, outs)
    residue_grad, pole_grad = small_call(
        partial(final_kernel, 1.0 / math.sqrt(total_tokens)),
        "parameter_grads",
        [rate, residue, gathered, swap_core(gathered)],
        [f32(modes, channels)] * 2,
        [pltpu.VMEM((2, rows, LANES), F32)] + [flat_scratch] * 2,
    )
    return (*(x[None] for x in outs), residue_grad, pole_grad)


def solution(mesh):
    tokens = P("dp", "ctx", None)
    return jax.shard_map(
        body,
        mesh=mesh,
        in_specs=(tokens, tokens, tokens, tokens, P(), P(), P("dp", None)),
        out_specs=(tokens, tokens, tokens, tokens, P(), P()),
        check_vma=False,
    )
```

```python
from functools import partial
import math

import jax
import jax.numpy as jnp
from jax import lax
from jax.experimental import pallas as pl
from jax.experimental.pallas import tpu as pltpu
from jax.sharding import PartitionSpec as P

F32 = jnp.float32
LANES = 128
SUBS = 8
GROUP = LANES * SUBS
CHUNK = 8
BIG = 32


def to_rows(left_ref, right_ref, rows_ref):
    tokens = left_ref.shape[0]
    for pair in range(tokens // 16):
        window = pl.ds(pair * 16, 16)
        for tile in range(SUBS):
            lanes = pl.ds(tile * LANES, LANES)
            product = left_ref[window, lanes].astype(F32) * right_ref[window, lanes].astype(F32)
            for part in range(2):
                start = (pair * 2 + part) * 64 + tile * 8
                rows_ref[pl.ds(start, 8), :] = product[part * 8 : part * 8 + 8]


def token_row(rows_ref, chunk, token):
    return rows_ref[pl.ds(chunk * 64 + token, 8, stride=8), :]


def mode_rows(natural_ref, rows_ref):
    for eight in range(natural_ref.shape[0] // 8):
        for tile in range(SUBS):
            rows_ref[pl.ds(eight * 64 + tile * 8, 8), :] = natural_ref[
                pl.ds(eight * 8, 8), pl.ds(tile * LANES, LANES)
            ]


def mode_row(rows_ref, mode):
    return rows_ref[pl.ds((mode // 8) * 64 + mode % 8, 8, stride=8), :]


def stats_kernel(
    row_len, k_ref, v_ref, q_ref, g_ref, pole_ref, c_ref, b_ref, rate_ref, kept_ref, send_ref,
    u_rows, d_rows, p_rows, lam_s, jump_s, slope_s, state_s, lag_s, res_s, mixl_s, head_s, headl_s, headm_s, pow_s,
    corr_s,
):
    modes = pole_ref.shape[0]
    chunks = k_ref.shape[0] // CHUNK
    first = lax.axis_index("ctx") % 2 == 0
    to_rows(k_ref, v_ref, u_rows)
    to_rows(g_ref, q_ref, d_rows)
    mode_rows(pole_ref, p_rows)
    zero = jnp.zeros((SUBS, LANES), F32)
    for m in range(modes):
        rate = mode_row(p_rows, m) / row_len
        rate_ref[0, m] = rate
        lam = jnp.exp(-rate)
        square = lam * lam
        fourth = square * square
        cube = square * lam
        for j, power in enumerate((lam, square, cube, fourth, fourth * lam, fourth * square, fourth * cube)):
            lam_s[m, j] = power
        jump_s[m] = fourth * fourth
        slope_s[m] = CHUNK * (fourth * fourth)
        for ref in (state_s, lag_s, res_s, mixl_s, head_s, headl_s, headm_s):
            ref[m] = zero
        pow_s[m] = zero + 1.0
    for lag in range(CHUNK):
        corr_s[lag] = zero

    def step(chunk, _):
        u = [token_row(u_rows, chunk, t) for t in range(CHUNK)]
        d = [token_row(d_rows, chunk, t) for t in range(CHUNK)]
        for lag in range(CHUNK):
            total = corr_s[lag]
            for t in range(CHUNK - lag):
                total = total + d[t + lag] * u[t]
            corr_s[lag] = total
        offset = (chunk * CHUNK).astype(F32)
        for m in range(modes):
            power = [lam_s[m, j] for j in range(CHUNK - 1)]
            end, head = power[-1] * u[0], power[-1] * d[-1]
            endl, headl = end, head
            for j in range(CHUNK - 2, 0, -1):
                end = end + power[j - 1] * u[CHUNK - 1 - j]
                endl = endl + end
                head = head + power[j - 1] * d[j]
                headl = headl + head
            end, head = end + u[-1], head + d[0]
            c_ref[0, chunk, m] = end
            b_ref[0, chunk, m] = head
            state, lag_state = state_s[m], lag_s[m]
            res_s[m] = res_s[m] + head * state
            mixl_s[m] = mixl_s[m] + (headl * state + head * lag_state)
            jump = jump_s[m]
            lag_s[m] = lag_state * jump + (state * slope_s[m] + endl)
            state_s[m] = state * jump + end
            decay = pow_s[m]
            far = decay * head
            head_s[m] = head_s[m] + far
            headl_s[m] = headl_s[m] + decay * headl
            headm_s[m] = headm_s[m] + offset * far
            pow_s[m] = decay * jump
        return 0

    lax.fori_loop(0, chunks, step, 0)
    def stats_of(m):
        lam = lam_s[m, 0]
        near, nearl = corr_s[CHUNK - 1], None
        for lag in range(CHUNK - 2, -1, -1):
            nearl = near if nearl is None else nearl * lam + near
            near = near * lam + corr_s[lag]
        res = res_s[m]
        return (
            state_s[m],
            lag_s[m],
            head_s[m],
            headl_s[m] + headm_s[m],
            near + lam * res,
            lam * (nearl + (res + mixl_s[m])),
        )

    half = modes // 2
    for m in range(half):
        kept_ref[6, 0, m] = jnp.where(first, rate_ref[0, m], rate_ref[0, m + half])
        for i, (low, high) in enumerate(zip(stats_of(m), stats_of(m + half))):
            kept_ref[i, 0, m] = jnp.where(first, low, high)
            send_ref[i, 0, m] = jnp.where(first, high, low)


def local_kernel(
    k_ref, v_ref, q_ref, g_ref, rate_ref, residue_ref, c_ref, b_ref, after_ref,
    z_ref, w_ref, zeros_ref, u_rows, d_rows, r_rows, lam_s, jump_s, lead_s, state_s, back_s, tap_s,
):
    modes = rate_ref.shape[1]
    chunks = k_ref.shape[0] // CHUNK
    zeros_ref[...] = jnp.zeros((1, LANES), F32)
    to_rows(k_ref, v_ref, u_rows)
    to_rows(g_ref, q_ref, d_rows)
    mode_rows(residue_ref, r_rows)
    zero = jnp.zeros((SUBS, LANES), F32)
    taps = [zero for _ in range(CHUNK)]
    for m in range(modes):
        rate = rate_ref[0, m]
        lam = jnp.exp(-rate)
        square = lam * lam
        fourth = square * square
        lam_s[m] = lam
        jump_s[m] = fourth * fourth
        power = mode_row(r_rows, m) * jnp.sqrt(2.0 * rate)
        lead_s[m] = power * lam
        for lag in range(CHUNK):
            taps[lag] = taps[lag] + power
            power = power * lam
        state_s[m] = zero
        back_s[m] = zero
    for lag in range(CHUNK):
        tap_s[lag] = taps[lag]

    def step(chunk, _):
        mirror = chunks - 1 - chunk
        u = [token_row(u_rows, chunk, t) for t in range(CHUNK)]
        z = [None] * CHUNK
        for lag in range(CHUNK):
            tap = tap_s[lag]
            for t in range(lag, CHUNK):
                term = tap * u[t - lag]
                z[t] = term if z[t] is None else z[t] + term
        d = [token_row(d_rows, mirror, t) for t in range(CHUNK)]
        w = [None] * CHUNK
        for lag in range(CHUNK):
            tap = tap_s[lag]
            for t in range(CHUNK - lag):
                term = tap * d[t + lag]
                w[t] = term if w[t] is None else w[t] + term
        for m in range(modes):
            lam, lead, jump = lam_s[m], lead_s[m], jump_s[m]
            state, back = state_s[m], back_s[m]
            ahead, behind = state * lead, back * lead
            for t in range(CHUNK):
                z[t] = z[t] + ahead
                w[CHUNK - 1 - t] = w[CHUNK - 1 - t] + behind
                if t + 1 < CHUNK:
                    ahead = ahead * lam
                    behind = behind * lam
            state_s[m] = state * jump + c_ref[0, chunk, m]
            back_s[m] = back * jump + b_ref[0, mirror, m]
        for t in range(CHUNK):
            z_ref[0, chunk * CHUNK + t] = z[t]
            w_ref[0, mirror * CHUNK + t] = w[t]
        return 0

    lax.fori_loop(0, chunks, step, 0)


def add_carry(group, chunks, core, rates, residues, edge, z_in, w_in, store, lam_s, ahead_s, behind_s):
    halves = lam_s.shape[0]
    for m in range(halves):
        rate = rates(core * halves + m)
        lam = jnp.exp(-rate)
        lam_s[m] = lam
        lead = residues(core, m) * jnp.sqrt(2.0 * rate) * lam
        ahead_s[m] = lead * edge(0, m)
        behind_s[m] = lead * edge(1, m)

    def step(chunk, _):
        mirror = chunks - 1 - chunk
        z = [z_in[group, chunk * CHUNK + t] for t in range(CHUNK)]
        w = [w_in[group, mirror * CHUNK + t] for t in range(CHUNK)]
        for m in range(halves):
            lam = lam_s[m]
            ahead, behind = ahead_s[m], behind_s[m]
            for t in range(CHUNK):
                z[t] = z[t] + ahead
                ahead = ahead * lam
                w[CHUNK - 1 - t] = w[CHUNK - 1 - t] + behind
                behind = behind * lam
            ahead_s[m] = ahead
            behind_s[m] = behind
        store(chunk, mirror, z, w)
        return 0

    lax.fori_loop(0, chunks, step, 0)


def output_kernel(
    earlier, k_ref, v_ref, q_ref, g_ref, rate_ref, residue_ref, zl_ref, wl_ref, got_ref, after_ref, *refs
):
    mixed_ref, qg_ref, kg_ref, vg_ref, zeros_ref = refs[earlier : earlier + 5]
    z_rows, w_rows, r_rows, lam_s, ahead_s, behind_s = refs[earlier + 5 :]
    chunks = k_ref.shape[0] // CHUNK
    zeros_ref[...] = jnp.zeros((1, LANES), F32)
    mode_rows(residue_ref, r_rows)

    def store(chunk, mirror, z, w):
        for t in range(CHUNK):
            z_rows[pl.ds(chunk * 64 + t, 8, stride=8), :] = z[t]
            w_rows[pl.ds(mirror * 64 + t, 8, stride=8), :] = w[t]

    add_carry(
        0, chunks, 1 - lax.axis_index("ctx") % 2, lambda mode: rate_ref[0, mode],
        lambda core, m: r_rows[pl.ds(core * 64 + m, 8, stride=8), :],
        lambda side, m: got_ref[side, 0, m], zl_ref, wl_ref, store, lam_s, ahead_s, behind_s,
    )
    for pair in range(chunks // 2):
        window = pl.ds(pair * 16, 16)
        for tile in range(SUBS):
            lanes = pl.ds(tile * LANES, LANES)
            z = jnp.concatenate([z_rows[pl.ds((pair * 2 + part) * 64 + tile * 8, 8), :] for part in range(2)], axis=0)
            w = jnp.concatenate([w_rows[pl.ds((pair * 2 + part) * 64 + tile * 8, 8), :] for part in range(2)], axis=0)
            mixed_ref[window, lanes] = (q_ref[window, lanes].astype(F32) * z).astype(jnp.bfloat16)
            qg_ref[window, lanes] = (g_ref[window, lanes].astype(F32) * z).astype(jnp.bfloat16)
            kg_ref[window, lanes] = (w * v_ref[window, lanes].astype(F32)).astype(jnp.bfloat16)
            vg_ref[window, lanes] = (w * k_ref[window, lanes].astype(F32)).astype(jnp.bfloat16)


def chip_of():
    me = lax.axis_index("ctx")
    return me % 2, me // 2


def joined_in(doc_ref, chip):
    return (doc_ref[0, 2 * chip] == doc_ref[0, 2 * chip + 1]).astype(F32)


def merge_kernel(block, chips, doc_ref, kept_ref, got_ref, *refs):
    outs, part_ref, chip_ref = refs[:chips], refs[chips], refs[chips + 1]
    core, chip = chip_of()
    first = core == 0
    half = kept_ref.shape[1]
    part = half // chips
    joined = joined_in(doc_ref, chip)
    rate = kept_ref[6]
    part_ref[...] = kept_ref[6, pl.ds(pl.multiple_of(chip * part, part), part), :]
    hop = joined * jnp.exp(-block * rate)
    link = joined * jnp.exp(-rate)
    left = [jnp.where(first, kept_ref[i], got_ref[i]) for i in range(6)]
    right = [jnp.where(first, got_ref[i], kept_ref[i]) for i in range(6)]
    chip_ref[0] = right[0] + hop * left[0]
    chip_ref[1] = right[1] + hop * (left[1] + block * left[0])
    chip_ref[2] = left[2] + hop * right[2]
    chip_ref[3] = left[3] + hop * (right[3] + block * right[2])
    chip_ref[4] = left[4] + right[4] + link * (right[2] * left[0])
    chip_ref[5] = left[5] + right[5] + link * ((right[3] + right[2]) * left[0] + right[2] * left[1])
    for away in range(chips):
        start = pl.multiple_of((chip ^ away) * part, part)
        outs[away][...] = chip_ref[:, pl.ds(start, part), :]


def scan_kernel(block, chips, doc_ref, rate_ref, *refs):
    refs = refs[:chips] + refs[chips + 1 :]
    ins, outs, total_ref = refs[:chips], refs[chips : 2 * chips], refs[2 * chips]
    ordered, ends = refs[2 * chips + 1], refs[2 * chips + 2]
    core, chip = chip_of()
    for away in range(chips):
        ordered[chip ^ away] = ins[away][...]
    rate = rate_ref[...]
    lam = jnp.exp(-rate)
    span = 2.0 * block
    hop = jnp.exp(-span * rate)
    zero = jnp.zeros_like(rate)
    state, lag_state, res, grad_lag = zero, zero, zero, zero
    for j in range(chips):
        ends[j, 0] = state
        res = res + (ordered[j, 4] + lam * (ordered[j, 2] * state))
        grad_lag = grad_lag + (
            ordered[j, 5]
            + lam * ((ordered[j, 3] + ordered[j, 2]) * state + ordered[j, 2] * lag_state)
        )
        if j + 1 < chips:
            through = joined_in(doc_ref, j) * hop
            keep = (doc_ref[0, 2 * j + 1] == doc_ref[0, 2 * j + 2]).astype(F32)
            lag_state = keep * (ordered[j, 1] + through * (lag_state + span * state))
            state = keep * (ordered[j, 0] + through * state)
    back = zero
    for j in range(chips - 1, -1, -1):
        ends[j, 1] = back
        if j > 0:
            through = joined_in(doc_ref, j) * hop
            keep = (doc_ref[0, 2 * j - 1] == doc_ref[0, 2 * j]).astype(F32)
            back = keep * (ordered[j, 2] + through * back)
    for away in range(chips):
        outs[away][...] = ends[chip ^ away]
    total_ref[0] = res
    total_ref[1] = grad_lag


def expand_kernel(block, chips, doc_ref, kept_ref, got_ref, rate_ref, residue_ref, z_in, w_in, *refs):
    ins, (send_ref, z_out, w_out), (whole, mine, r_rows, lam_s, ahead_s, behind_s) = (
        refs[:chips], refs[chips : chips + 3], refs[chips + 3 :],
    )
    core, chip = chip_of()
    first = core == 0
    joined = joined_in(doc_ref, chip)
    part = ins[0].shape[1]
    for away in range(chips):
        start = pl.multiple_of((chip ^ away) * part, part)
        whole[:, pl.ds(start, part), :] = ins[away][...]
    hop = joined * jnp.exp(-block * kept_ref[6])
    end_left = jnp.where(first, kept_ref[0], got_ref[0])
    head_right = jnp.where(first, got_ref[2], kept_ref[2])
    state, back = whole[0], whole[1]
    state_right = joined * end_left + hop * state
    back_left = joined * head_right + hop * back
    mine[0] = jnp.where(first, state, state_right)
    mine[1] = jnp.where(first, back_left, back)
    send_ref[0] = jnp.where(first, state_right, state)
    send_ref[1] = jnp.where(first, back, back_left)
    groups, tokens = z_in.shape[0], z_in.shape[1]
    halves = lam_s.shape[0]

    def one_group(group, _):
        modes = pl.ds(pl.multiple_of(core * halves, halves), halves)
        for tile in range(SUBS):
            lanes = pl.ds(pl.multiple_of(group * GROUP + tile * LANES, LANES), LANES)
            r_rows[pl.ds(tile * 8, 8), :] = residue_ref[modes, lanes]

        def store(chunk, mirror, z, w):
            for t in range(CHUNK):
                z_out[group, chunk * CHUNK + t] = z[t]
                w_out[group, mirror * CHUNK + t] = w[t]

        add_carry(
            group, tokens // CHUNK, core, lambda mode: rate_ref[group, mode],
            lambda core, m: r_rows[pl.ds(m, 8, stride=8), :],
            lambda side, m: mine[side, pl.ds(pl.multiple_of((group * halves + m) * SUBS, SUBS), SUBS), :],
            z_in, w_in, store, lam_s, ahead_s, behind_s,
        )
        return 0

    lax.fori_loop(0, groups, one_group, 0)


def gather_kernel(chips, *refs):
    ins, out_ref = refs[:chips], refs[chips + 1]
    core, chip = chip_of()
    part = ins[0].shape[1]
    for away in range(chips):
        start = pl.multiple_of((chip ^ away) * part, part)
        out_ref[:, pl.ds(start, part), :] = ins[away][...]


def final_kernel(scale, rate_ref, residue_ref, kept_ref, got_ref, res_ref, grad_ref, sums, res_rows, grad_rows):
    core, chip = chip_of()
    half = kept_ref.shape[1]
    sums[:, pl.ds(pl.multiple_of(core * half, half), half), :] = kept_ref[...]
    sums[:, pl.ds(pl.multiple_of((1 - core) * half, half), half), :] = got_ref[...]
    modes, channels = residue_ref.shape
    halves = modes // 2
    for group in range(channels // GROUP):
        for m in range(modes):
            window = pl.ds((m // halves) * half + (group * halves + m % halves) * SUBS, SUBS)
            rate = rate_ref[group, m]
            root = jnp.sqrt(2.0 * rate) * scale
            grad_res, grad_lag = sums[0, window, :], sums[1, window, :]
            target = pl.ds((m // 8) * 64 + m % 8, 8, stride=8)
            res_rows[target, :] = root * grad_res
            grad_rows[target, :] = root * (0.5 * grad_res - rate * grad_lag)
        for eight in range(modes // 8):
            for tile in range(SUBS):
                place = (pl.ds(eight * 8, 8), pl.ds(group * GROUP + tile * LANES, LANES))
                rows = pl.ds(eight * 64 + tile * 8, 8)
                res_ref[place] = res_rows[rows, :]
                grad_ref[place] = residue_ref[place] * grad_rows[rows, :]


def whole(array):
    rank = len(array.shape)
    return pl.BlockSpec(array.shape, lambda i: (0,) * rank)


def unread():
    return pl.BlockSpec(memory_space=pl.ANY)


def small_call(kernel, name, ins, outs, scratch, after=()):
    return pl.pallas_call(
        kernel,
        grid=(1,),
        in_specs=[scalar_spec() if x.dtype == jnp.int32 else whole(x) for x in ins] + [unread() for _ in after],
        out_specs=[whole(x) for x in outs],
        out_shape=outs,
        scratch_shapes=scratch,
        compiler_params=params(),
        name=name,
    )(*ins, *after)


def hbm(x):
    return pltpu.with_memory_space_constraint(x, pltpu.HBM)


def vmem(x):
    return pltpu.with_memory_space_constraint(x, pltpu.VMEM)


def f32(*shape):
    return jax.ShapeDtypeStruct(shape, F32)


def scalar_spec():
    return pl.BlockSpec(memory_space=pltpu.SMEM)


def params(mib=16):
    return pltpu.CompilerParams(vmem_limit_bytes=mib * 1024 * 1024)


def body(q_proj, k_proj, v_proj, out_grad, residue, pole_decay, group_doc):
    block, channels = q_proj.shape[1], q_proj.shape[2]
    modes = residue.shape[0]
    n_ctx, n_dp = lax.axis_size("ctx"), lax.axis_size("dp")
    row_len = block * n_ctx
    total_tokens = row_len * n_dp
    chips = n_ctx // 2
    groups = channels // GROUP
    chunks = block // CHUNK
    rows = modes * channels // LANES
    half = rows // 2
    part = half // chips
    halves = modes // 2

    tokens = [x.reshape(block, channels) for x in (k_proj, v_proj, q_proj, out_grad)]
    k_in, v_in, q_in, g_in = (hbm(x) for x in tokens)
    row_scratch = pltpu.VMEM((block * SUBS, LANES), F32)
    mode_scratch = pltpu.VMEM((modes, SUBS, LANES), F32)
    flat_scratch = pltpu.VMEM((modes * SUBS, LANES), F32)
    tap_scratch = pltpu.VMEM((CHUNK, SUBS, LANES), F32)

    def specs(at):
        return (
            pl.BlockSpec((block, GROUP), lambda i: (0, at(i))),
            pl.BlockSpec((1, modes, SUBS, LANES), lambda i: (at(i), 0, 0, 0)),
            pl.BlockSpec((modes, GROUP), lambda i: (0, at(i))),
            pl.BlockSpec((1, chunks, modes, SUBS, LANES), lambda i: (at(i), 0, 0, 0, 0)),
            lambda count: pl.BlockSpec((count, 1, halves, SUBS, LANES), lambda i: (0, at(i), 0, 0, 0)),
        )

    wide, slim, natural, chunked, halved = specs(lambda i: i)
    ends, heads, rate, kept, send = pl.pallas_call(
        partial(stats_kernel, float(row_len)),
        grid=(groups,),
        in_specs=[wide] * 4 + [natural],
        out_specs=[chunked, chunked, slim, halved(7), halved(6)],
        out_shape=[
            pltpu.VMEM((groups, chunks, modes, SUBS, LANES), F32),
            pltpu.VMEM((groups, chunks, modes, SUBS, LANES), F32),
            pltpu.VMEM((groups, modes, SUBS, LANES), F32),
            pltpu.VMEM((7, groups, halves, SUBS, LANES), F32),
            pltpu.VMEM((6, groups, halves, SUBS, LANES), F32),
        ],
        scratch_shapes=[row_scratch] * 2 + [flat_scratch, pltpu.VMEM((modes, CHUNK - 1, SUBS, LANES), F32)]
        + [mode_scratch] * 10 + [tap_scratch],
        compiler_params=params(BIG),
        name="block_stats",
    )(k_in, v_in, q_in, g_in, hbm(pole_decay))

    kept = kept.reshape(7, half, LANES)
    send = send.reshape(6, half, LANES)

    def swap_core(x):
        return lax.ppermute(x, "ctx", [(i, i ^ 1) for i in range(n_ctx)])

    def swap_chips(xs):
        return [xs[0]] + [
            lax.ppermute(xs[away], "ctx", [(i, i ^ (2 * away)) for i in range(n_ctx)]) for away in range(1, chips)
        ]

    got = swap_core(send)
    *pieces, rate_part = small_call(
        partial(merge_kernel, float(block), chips),
        "chip_stats",
        [group_doc, kept, got],
        [f32(6, part, LANES)] * chips + [f32(part, LANES)],
        [pltpu.VMEM((6, half, LANES), F32)],
    )
    columns = pl.BlockSpec((1, block, SUBS, LANES), lambda i: (i, 0, 0, 0))
    z_local, w_local, zeros = pl.pallas_call(
        local_kernel,
        grid=(groups,),
        in_specs=[wide] * 4 + [slim, natural] + [chunked] * 2 + [pl.BlockSpec(memory_space=pl.ANY)],
        out_specs=[columns] * 2 + [pl.BlockSpec((1, LANES), lambda i: (0, 0))],
        out_shape=[pltpu.VMEM((groups, block, SUBS, LANES), F32)] * 2 + [pltpu.VMEM((1, LANES), F32)],
        scratch_shapes=[row_scratch] * 2 + [flat_scratch] + [mode_scratch] * 5 + [tap_scratch],
        compiler_params=params(BIG),
        cost_estimate=pl.CostEstimate(flops=10_000_000_000, bytes_accessed=20_000_000, transcendentals=0),
        name="local_outputs",
    )(k_in, v_in, q_in, g_in, vmem(rate), hbm(residue), vmem(ends), vmem(heads), rate_part)
    scanned = small_call(
        partial(scan_kernel, float(block), chips),
        "row_scan",
        [group_doc, rate_part, *swap_chips(pieces)],
        [f32(2, part, LANES)] * (chips + 1),
        [pltpu.VMEM((chips, 6, part, LANES), F32), pltpu.VMEM((chips, 2, part, LANES), F32)],
        after=[zeros],
    )
    total = scanned[chips]
    for other in [lax.ppermute(total, "dp", [(i, i ^ away) for i in range(n_dp)]) for away in range(1, n_dp)]:
        total = total + other
    held = [vmem(x) for x in (*tokens, rate, residue)]
    half_scratch = pltpu.VMEM((halves, SUBS, LANES), F32)
    in_vmem = pl.BlockSpec(memory_space=pltpu.VMEM)
    give, z_local, w_local = pl.pallas_call(
        partial(expand_kernel, float(block), chips),
        in_specs=[scalar_spec()] + [in_vmem] * (6 + chips),
        out_specs=[in_vmem] * 3,
        out_shape=[f32(2, half, LANES)] + [f32(groups, block, SUBS, LANES)] * 2,
        input_output_aliases={5: 1, 6: 2},
        scratch_shapes=[pltpu.VMEM((2, half, LANES), F32)] * 2
        + [pltpu.VMEM((GROUP // LANES * halves, LANES), F32)] + [half_scratch] * 3,
        compiler_params=params(),
        name="block_edges",
    )(group_doc, kept, got, rate, residue, z_local, w_local, *swap_chips(scanned[:chips]))
    theirs = swap_core(give).reshape(2, groups, halves, SUBS, LANES)

    def outputs(first, count, after, outs):
        wide, slim, natural, chunked, halved = specs(lambda i: i + first)
        columns = pl.BlockSpec((1, block, SUBS, LANES), lambda i: (i + first, 0, 0, 0))
        result = pl.pallas_call(
            partial(output_kernel, len(outs)),
            grid=(count,),
            in_specs=[wide] * 4 + [slim, natural] + [columns] * 2 + [halved(2)]
            + [pl.BlockSpec(memory_space=pl.ANY)] * (1 + len(outs)),
            out_specs=[wide] * 4 + [pl.BlockSpec((1, LANES), lambda i: (0, 0))],
            out_shape=[pltpu.HBM((block, channels), jnp.bfloat16)] * 4 + [pltpu.VMEM((1, LANES), F32)],
            input_output_aliases={10 + i: i for i in range(len(outs))},
            scratch_shapes=[row_scratch] * 2 + [flat_scratch] + [half_scratch] * 3,
            compiler_params=params(BIG),
            cost_estimate=pl.CostEstimate(
                flops=100_000_000 * count, bytes_accessed=500_000 * count, transcendentals=0
            ),
            name="outputs",
        )(*held, vmem(z_local), vmem(w_local), theirs, after, *outs)
        return result[:4], result[4]

    sums = swap_chips([total] * chips)
    cut = (3 * groups + 3) // 4
    outs, zeros = outputs(0, cut, total, [])
    (gathered,) = small_call(
        partial(gather_kernel, chips), "gather_sums", sums, [f32(2, half, LANES)], [], after=[zeros]
    )
    if cut < groups:
        outs, _ = outputs(cut, groups - cut, gathered, outs)
    residue_grad, pole_grad = small_call(
        partial(final_kernel, 1.0 / math.sqrt(total_tokens)),
        "parameter_grads",
        [rate, residue, gathered, swap_core(gathered)],
        [f32(modes, channels)] * 2,
        [pltpu.VMEM((2, rows, LANES), F32)] + [flat_scratch] * 2,
    )
    return (*(x[None] for x in outs), residue_grad, pole_grad)


def solution(mesh):
    tokens = P("dp", "ctx", None)
    return jax.shard_map(
        body,
        mesh=mesh,
        in_specs=(tokens, tokens, tokens, tokens, P(), P(), P("dp", None)),
        out_specs=(tokens, tokens, tokens, tokens, P(), P()),
        check_vma=False,
    )
```

```python
from functools import partial
import math

import jax
import jax.numpy as jnp
from jax import lax
from jax.experimental import pallas as pl
from jax.experimental.pallas import tpu as pltpu
from jax.sharding import PartitionSpec as P

F32 = jnp.float32
LANES = 128
SUBS = 8
GROUP = LANES * SUBS
CHUNK = 8
BIG = 32


def to_rows(left_ref, right_ref, rows_ref):
    tokens = left_ref.shape[0]
    for pair in range(tokens // 16):
        window = pl.ds(pair * 16, 16)
        for tile in range(SUBS):
            lanes = pl.ds(tile * LANES, LANES)
            product = left_ref[window, lanes].astype(F32) * right_ref[window, lanes].astype(F32)
            for part in range(2):
                start = (pair * 2 + part) * 64 + tile * 8
                rows_ref[pl.ds(start, 8), :] = product[part * 8 : part * 8 + 8]


def token_row(rows_ref, chunk, token):
    return rows_ref[pl.ds(chunk * 64 + token, 8, stride=8), :]


def mode_rows(natural_ref, rows_ref):
    for eight in range(natural_ref.shape[0] // 8):
        for tile in range(SUBS):
            rows_ref[pl.ds(eight * 64 + tile * 8, 8), :] = natural_ref[
                pl.ds(eight * 8, 8), pl.ds(tile * LANES, LANES)
            ]


def mode_row(rows_ref, mode):
    return rows_ref[pl.ds((mode // 8) * 64 + mode % 8, 8, stride=8), :]


def stats_kernel(
    row_len, k_ref, v_ref, q_ref, g_ref, pole_ref, c_ref, b_ref, rate_ref, kept_ref, send_ref,
    u_rows, d_rows, p_rows, lam_s, jump_s, slope_s, state_s, lag_s, res_s, mixl_s, head_s, headl_s, headm_s, pow_s,
    corr_s,
):
    modes = pole_ref.shape[0]
    chunks = k_ref.shape[0] // CHUNK
    first = lax.axis_index("ctx") % 2 == 0
    to_rows(k_ref, v_ref, u_rows)
    to_rows(g_ref, q_ref, d_rows)
    mode_rows(pole_ref, p_rows)
    zero = jnp.zeros((SUBS, LANES), F32)
    for m in range(modes):
        rate = mode_row(p_rows, m) / row_len
        rate_ref[0, m] = rate
        lam = jnp.exp(-rate)
        square = lam * lam
        fourth = square * square
        cube = square * lam
        for j, power in enumerate((lam, square, cube, fourth, fourth * lam, fourth * square, fourth * cube)):
            lam_s[m, j] = power
        jump_s[m] = fourth * fourth
        slope_s[m] = CHUNK * (fourth * fourth)
        for ref in (state_s, lag_s, res_s, mixl_s, head_s, headl_s, headm_s):
            ref[m] = zero
        pow_s[m] = zero + 1.0
    for lag in range(CHUNK):
        corr_s[lag] = zero

    def step(chunk, _):
        u = [token_row(u_rows, chunk, t) for t in range(CHUNK)]
        d = [token_row(d_rows, chunk, t) for t in range(CHUNK)]
        for lag in range(CHUNK):
            total = corr_s[lag]
            for t in range(CHUNK - lag):
                total = total + d[t + lag] * u[t]
            corr_s[lag] = total
        offset = (chunk * CHUNK).astype(F32)
        for m in range(modes):
            power = [lam_s[m, j] for j in range(CHUNK - 1)]
            end, head = power[-1] * u[0], power[-1] * d[-1]
            endl, headl = end, head
            for j in range(CHUNK - 2, 0, -1):
                end = end + power[j - 1] * u[CHUNK - 1 - j]
                endl = endl + end
                head = head + power[j - 1] * d[j]
                headl = headl + head
            end, head = end + u[-1], head + d[0]
            c_ref[0, chunk, m] = end
            b_ref[0, chunk, m] = head
            state, lag_state = state_s[m], lag_s[m]
            res_s[m] = res_s[m] + head * state
            mixl_s[m] = mixl_s[m] + (headl * state + head * lag_state)
            jump = jump_s[m]
            lag_s[m] = lag_state * jump + (state * slope_s[m] + endl)
            state_s[m] = state * jump + end
            decay = pow_s[m]
            far = decay * head
            head_s[m] = head_s[m] + far
            headl_s[m] = headl_s[m] + decay * headl
            headm_s[m] = headm_s[m] + offset * far
            pow_s[m] = decay * jump
        return 0

    lax.fori_loop(0, chunks, step, 0)
    def stats_of(m):
        lam = lam_s[m, 0]
        near, nearl = corr_s[CHUNK - 1], None
        for lag in range(CHUNK - 2, -1, -1):
            nearl = near if nearl is None else nearl * lam + near
            near = near * lam + corr_s[lag]
        res = res_s[m]
        return (
            state_s[m],
            lag_s[m],
            head_s[m],
            headl_s[m] + headm_s[m],
            near + lam * res,
            lam * (nearl + (res + mixl_s[m])),
        )

    half = modes // 2
    for m in range(half):
        kept_ref[6, 0, m] = jnp.where(first, rate_ref[0, m], rate_ref[0, m + half])
        for i, (low, high) in enumerate(zip(stats_of(m), stats_of(m + half))):
            kept_ref[i, 0, m] = jnp.where(first, low, high)
            send_ref[i, 0, m] = jnp.where(first, high, low)


def local_kernel(
    k_ref, v_ref, q_ref, g_ref, rate_ref, residue_ref, c_ref, b_ref, after_ref,
    z_ref, w_ref, zeros_ref, u_rows, d_rows, r_rows, lam_s, jump_s, lead_s, state_s, back_s, tap_s,
):
    modes = rate_ref.shape[1]
    chunks = k_ref.shape[0] // CHUNK
    zeros_ref[...] = jnp.zeros((1, LANES), F32)
    to_rows(k_ref, v_ref, u_rows)
    to_rows(g_ref, q_ref, d_rows)
    mode_rows(residue_ref, r_rows)
    zero = jnp.zeros((SUBS, LANES), F32)
    taps = [zero for _ in range(CHUNK)]
    for m in range(modes):
        rate = rate_ref[0, m]
        lam = jnp.exp(-rate)
        square = lam * lam
        fourth = square * square
        lam_s[m] = lam
        jump_s[m] = fourth * fourth
        power = mode_row(r_rows, m) * jnp.sqrt(2.0 * rate)
        lead_s[m] = power * lam
        for lag in range(CHUNK):
            taps[lag] = taps[lag] + power
            power = power * lam
        state_s[m] = zero
        back_s[m] = zero
    for lag in range(CHUNK):
        tap_s[lag] = taps[lag]

    def step(chunk, _):
        mirror = chunks - 1 - chunk
        u = [token_row(u_rows, chunk, t) for t in range(CHUNK)]
        z = [None] * CHUNK
        for lag in range(CHUNK):
            tap = tap_s[lag]
            for t in range(lag, CHUNK):
                term = tap * u[t - lag]
                z[t] = term if z[t] is None else z[t] + term
        d = [token_row(d_rows, mirror, t) for t in range(CHUNK)]
        w = [None] * CHUNK
        for lag in range(CHUNK):
            tap = tap_s[lag]
            for t in range(CHUNK - lag):
                term = tap * d[t + lag]
                w[t] = term if w[t] is None else w[t] + term
        for m in range(modes):
            lam, lead, jump = lam_s[m], lead_s[m], jump_s[m]
            state, back = state_s[m], back_s[m]
            ahead, behind = state * lead, back * lead
            for t in range(CHUNK):
                z[t] = z[t] + ahead
                w[CHUNK - 1 - t] = w[CHUNK - 1 - t] + behind
                if t + 1 < CHUNK:
                    ahead = ahead * lam
                    behind = behind * lam
            state_s[m] = state * jump + c_ref[0, chunk, m]
            back_s[m] = back * jump + b_ref[0, mirror, m]
        for t in range(CHUNK):
            z_ref[0, chunk * CHUNK + t] = z[t]
            w_ref[0, mirror * CHUNK + t] = w[t]
        return 0

    lax.fori_loop(0, chunks, step, 0)


def add_carry(group, chunks, core, rates, residues, edge, z_in, w_in, store, lam_s, ahead_s, behind_s):
    halves = lam_s.shape[0]
    for m in range(halves):
        rate = rates(core * halves + m)
        lam = jnp.exp(-rate)
        lam_s[m] = lam
        lead = residues(core, m) * jnp.sqrt(2.0 * rate) * lam
        ahead_s[m] = lead * edge(0, m)
        behind_s[m] = lead * edge(1, m)

    def step(chunk, _):
        mirror = chunks - 1 - chunk
        z = [z_in[group, chunk * CHUNK + t] for t in range(CHUNK)]
        w = [w_in[group, mirror * CHUNK + t] for t in range(CHUNK)]
        for m in range(halves):
            lam = lam_s[m]
            ahead, behind = ahead_s[m], behind_s[m]
            for t in range(CHUNK):
                z[t] = z[t] + ahead
                ahead = ahead * lam
                w[CHUNK - 1 - t] = w[CHUNK - 1 - t] + behind
                behind = behind * lam
            ahead_s[m] = ahead
            behind_s[m] = behind
        store(chunk, mirror, z, w)
        return 0

    lax.fori_loop(0, chunks, step, 0)


def output_kernel(
    earlier, k_ref, v_ref, q_ref, g_ref, rate_ref, residue_ref, zl_ref, wl_ref, got_ref, after_ref, *refs
):
    mixed_ref, qg_ref, kg_ref, vg_ref, zeros_ref = refs[earlier : earlier + 5]
    z_rows, w_rows, r_rows, lam_s, ahead_s, behind_s = refs[earlier + 5 :]
    chunks = k_ref.shape[0] // CHUNK
    zeros_ref[...] = jnp.zeros((1, LANES), F32)
    mode_rows(residue_ref, r_rows)

    def store(chunk, mirror, z, w):
        for t in range(CHUNK):
            z_rows[pl.ds(chunk * 64 + t, 8, stride=8), :] = z[t]
            w_rows[pl.ds(mirror * 64 + t, 8, stride=8), :] = w[t]

    add_carry(
        0, chunks, 1 - lax.axis_index("ctx") % 2, lambda mode: rate_ref[0, mode],
        lambda core, m: r_rows[pl.ds(core * 64 + m, 8, stride=8), :],
        lambda side, m: got_ref[side, 0, m], zl_ref, wl_ref, store, lam_s, ahead_s, behind_s,
    )
    for pair in range(chunks // 2):
        window = pl.ds(pair * 16, 16)
        for tile in range(SUBS):
            lanes = pl.ds(tile * LANES, LANES)
            z = jnp.concatenate([z_rows[pl.ds((pair * 2 + part) * 64 + tile * 8, 8), :] for part in range(2)], axis=0)
            w = jnp.concatenate([w_rows[pl.ds((pair * 2 + part) * 64 + tile * 8, 8), :] for part in range(2)], axis=0)
            mixed_ref[window, lanes] = (q_ref[window, lanes].astype(F32) * z).astype(jnp.bfloat16)
            qg_ref[window, lanes] = (g_ref[window, lanes].astype(F32) * z).astype(jnp.bfloat16)
            kg_ref[window, lanes] = (w * v_ref[window, lanes].astype(F32)).astype(jnp.bfloat16)
            vg_ref[window, lanes] = (w * k_ref[window, lanes].astype(F32)).astype(jnp.bfloat16)


def chip_of():
    me = lax.axis_index("ctx")
    return me % 2, me // 2


def joined_in(doc_ref, chip):
    return (doc_ref[0, 2 * chip] == doc_ref[0, 2 * chip + 1]).astype(F32)


def merge_kernel(block, chips, doc_ref, kept_ref, got_ref, *refs):
    outs, part_ref = refs[:chips], refs[chips]
    core, chip = chip_of()
    first = core == 0
    half = kept_ref.shape[1]
    part = half // chips
    joined = joined_in(doc_ref, chip)
    part_ref[...] = kept_ref[6, pl.ds(pl.multiple_of(chip * part, part), part), :]
    for away in range(chips):
        rows = pl.ds(pl.multiple_of((chip ^ away) * part, part), part)
        out = outs[away]
        rate = kept_ref[6, rows, :]
        hop = joined * jnp.exp(-block * rate)
        link = joined * jnp.exp(-rate)
        left = [jnp.where(first, kept_ref[i, rows, :], got_ref[i, rows, :]) for i in range(6)]
        right = [jnp.where(first, got_ref[i, rows, :], kept_ref[i, rows, :]) for i in range(6)]
        out[0] = right[0] + hop * left[0]
        out[1] = right[1] + hop * (left[1] + block * left[0])
        out[2] = left[2] + hop * right[2]
        out[3] = left[3] + hop * (right[3] + block * right[2])
        out[4] = left[4] + right[4] + link * (right[2] * left[0])
        out[5] = left[5] + right[5] + link * ((right[3] + right[2]) * left[0] + right[2] * left[1])


def scan_kernel(block, chips, doc_ref, rate_ref, *refs):
    refs = refs[:chips] + refs[chips + 1 :]
    ins, outs, total_ref = refs[:chips], refs[chips : 2 * chips], refs[2 * chips]
    ordered, ends = refs[2 * chips + 1], refs[2 * chips + 2]
    core, chip = chip_of()
    for away in range(chips):
        ordered[chip ^ away] = ins[away][...]
    rate = rate_ref[...]
    lam = jnp.exp(-rate)
    span = 2.0 * block
    hop = jnp.exp(-span * rate)
    zero = jnp.zeros_like(rate)
    state, lag_state, res, grad_lag = zero, zero, zero, zero
    for j in range(chips):
        ends[j, 0] = state
        res = res + (ordered[j, 4] + lam * (ordered[j, 2] * state))
        grad_lag = grad_lag + (
            ordered[j, 5]
            + lam * ((ordered[j, 3] + ordered[j, 2]) * state + ordered[j, 2] * lag_state)
        )
        if j + 1 < chips:
            through = joined_in(doc_ref, j) * hop
            keep = (doc_ref[0, 2 * j + 1] == doc_ref[0, 2 * j + 2]).astype(F32)
            lag_state = keep * (ordered[j, 1] + through * (lag_state + span * state))
            state = keep * (ordered[j, 0] + through * state)
    back = zero
    for j in range(chips - 1, -1, -1):
        ends[j, 1] = back
        if j > 0:
            through = joined_in(doc_ref, j) * hop
            keep = (doc_ref[0, 2 * j - 1] == doc_ref[0, 2 * j]).astype(F32)
            back = keep * (ordered[j, 2] + through * back)
    for away in range(chips):
        outs[away][...] = ends[chip ^ away]
    total_ref[0] = res
    total_ref[1] = grad_lag


def expand_kernel(block, chips, doc_ref, kept_ref, got_ref, rate_ref, residue_ref, z_in, w_in, *refs):
    ins, (send_ref, z_out, w_out), (whole, mine, r_rows, lam_s, ahead_s, behind_s) = (
        refs[:chips], refs[chips : chips + 3], refs[chips + 3 :],
    )
    core, chip = chip_of()
    first = core == 0
    joined = joined_in(doc_ref, chip)
    part = ins[0].shape[1]
    for away in range(chips):
        start = pl.multiple_of((chip ^ away) * part, part)
        whole[:, pl.ds(start, part), :] = ins[away][...]
    hop = joined * jnp.exp(-block * kept_ref[6])
    end_left = jnp.where(first, kept_ref[0], got_ref[0])
    head_right = jnp.where(first, got_ref[2], kept_ref[2])
    state, back = whole[0], whole[1]
    state_right = joined * end_left + hop * state
    back_left = joined * head_right + hop * back
    mine[0] = jnp.where(first, state, state_right)
    mine[1] = jnp.where(first, back_left, back)
    send_ref[0] = jnp.where(first, state_right, state)
    send_ref[1] = jnp.where(first, back, back_left)
    groups, tokens = z_in.shape[0], z_in.shape[1]
    halves = lam_s.shape[0]

    def one_group(group, _):
        modes = pl.ds(pl.multiple_of(core * halves, halves), halves)
        for tile in range(SUBS):
            lanes = pl.ds(pl.multiple_of(group * GROUP + tile * LANES, LANES), LANES)
            r_rows[pl.ds(tile * 8, 8), :] = residue_ref[modes, lanes]

        def store(chunk, mirror, z, w):
            for t in range(CHUNK):
                z_out[group, chunk * CHUNK + t] = z[t]
                w_out[group, mirror * CHUNK + t] = w[t]

        add_carry(
            group, tokens // CHUNK, core, lambda mode: rate_ref[group, mode],
            lambda core, m: r_rows[pl.ds(m, 8, stride=8), :],
            lambda side, m: mine[side, pl.ds(pl.multiple_of((group * halves + m) * SUBS, SUBS), SUBS), :],
            z_in, w_in, store, lam_s, ahead_s, behind_s,
        )
        return 0

    lax.fori_loop(0, groups, one_group, 0)


def gather_kernel(chips, *refs):
    ins, out_ref = refs[:chips], refs[chips + 1]
    core, chip = chip_of()
    part = ins[0].shape[1]
    for away in range(chips):
        start = pl.multiple_of((chip ^ away) * part, part)
        out_ref[:, pl.ds(start, part), :] = ins[away][...]


def final_kernel(scale, rate_ref, residue_ref, kept_ref, got_ref, res_ref, grad_ref, sums, res_rows, grad_rows):
    core, chip = chip_of()
    half = kept_ref.shape[1]
    sums[:, pl.ds(pl.multiple_of(core * half, half), half), :] = kept_ref[...]
    sums[:, pl.ds(pl.multiple_of((1 - core) * half, half), half), :] = got_ref[...]
    modes, channels = residue_ref.shape
    halves = modes // 2
    for group in range(channels // GROUP):
        for m in range(modes):
            window = pl.ds((m // halves) * half + (group * halves + m % halves) * SUBS, SUBS)
            rate = rate_ref[group, m]
            root = jnp.sqrt(2.0 * rate) * scale
            grad_res, grad_lag = sums[0, window, :], sums[1, window, :]
            target = pl.ds((m // 8) * 64 + m % 8, 8, stride=8)
            res_rows[target, :] = root * grad_res
            grad_rows[target, :] = root * (0.5 * grad_res - rate * grad_lag)
        for eight in range(modes // 8):
            for tile in range(SUBS):
                place = (pl.ds(eight * 8, 8), pl.ds(group * GROUP + tile * LANES, LANES))
                rows = pl.ds(eight * 64 + tile * 8, 8)
                res_ref[place] = res_rows[rows, :]
                grad_ref[place] = residue_ref[place] * grad_rows[rows, :]


def whole(array):
    rank = len(array.shape)
    return pl.BlockSpec(array.shape, lambda i: (0,) * rank)


def unread():
    return pl.BlockSpec(memory_space=pl.ANY)


def small_call(kernel, name, ins, outs, scratch, after=()):
    return pl.pallas_call(
        kernel,
        grid=(1,),
        in_specs=[scalar_spec() if x.dtype == jnp.int32 else whole(x) for x in ins] + [unread() for _ in after],
        out_specs=[whole(x) for x in outs],
        out_shape=outs,
        scratch_shapes=scratch,
        compiler_params=params(),
        name=name,
    )(*ins, *after)


def hbm(x):
    return pltpu.with_memory_space_constraint(x, pltpu.HBM)


def vmem(x):
    return pltpu.with_memory_space_constraint(x, pltpu.VMEM)


def f32(*shape):
    return jax.ShapeDtypeStruct(shape, F32)


def scalar_spec():
    return pl.BlockSpec(memory_space=pltpu.SMEM)


def params(mib=16):
    return pltpu.CompilerParams(vmem_limit_bytes=mib * 1024 * 1024)


def body(q_proj, k_proj, v_proj, out_grad, residue, pole_decay, group_doc):
    block, channels = q_proj.shape[1], q_proj.shape[2]
    modes = residue.shape[0]
    n_ctx, n_dp = lax.axis_size("ctx"), lax.axis_size("dp")
    row_len = block * n_ctx
    total_tokens = row_len * n_dp
    chips = n_ctx // 2
    groups = channels // GROUP
    chunks = block // CHUNK
    rows = modes * channels // LANES
    half = rows // 2
    part = half // chips
    halves = modes // 2

    tokens = [x.reshape(block, channels) for x in (k_proj, v_proj, q_proj, out_grad)]
    k_in, v_in, q_in, g_in = (hbm(x) for x in tokens)
    row_scratch = pltpu.VMEM((block * SUBS, LANES), F32)
    mode_scratch = pltpu.VMEM((modes, SUBS, LANES), F32)
    flat_scratch = pltpu.VMEM((modes * SUBS, LANES), F32)
    tap_scratch = pltpu.VMEM((CHUNK, SUBS, LANES), F32)

    def specs(at):
        return (
            pl.BlockSpec((block, GROUP), lambda i: (0, at(i))),
            pl.BlockSpec((1, modes, SUBS, LANES), lambda i: (at(i), 0, 0, 0)),
            pl.BlockSpec((modes, GROUP), lambda i: (0, at(i))),
            pl.BlockSpec((1, chunks, modes, SUBS, LANES), lambda i: (at(i), 0, 0, 0, 0)),
            lambda count: pl.BlockSpec((count, 1, halves, SUBS, LANES), lambda i: (0, at(i), 0, 0, 0)),
        )

    wide, slim, natural, chunked, halved = specs(lambda i: i)
    ends, heads, rate, kept, send = pl.pallas_call(
        partial(stats_kernel, float(row_len)),
        grid=(groups,),
        in_specs=[wide] * 4 + [natural],
        out_specs=[chunked, chunked, slim, halved(7), halved(6)],
        out_shape=[
            pltpu.VMEM((groups, chunks, modes, SUBS, LANES), F32),
            pltpu.VMEM((groups, chunks, modes, SUBS, LANES), F32),
            pltpu.VMEM((groups, modes, SUBS, LANES), F32),
            pltpu.VMEM((7, groups, halves, SUBS, LANES), F32),
            pltpu.VMEM((6, groups, halves, SUBS, LANES), F32),
        ],
        scratch_shapes=[row_scratch] * 2 + [flat_scratch, pltpu.VMEM((modes, CHUNK - 1, SUBS, LANES), F32)]
        + [mode_scratch] * 10 + [tap_scratch],
        compiler_params=params(BIG),
        name="block_stats",
    )(k_in, v_in, q_in, g_in, hbm(pole_decay))

    kept = kept.reshape(7, half, LANES)
    send = send.reshape(6, half, LANES)

    def swap_core(x):
        return lax.ppermute(x, "ctx", [(i, i ^ 1) for i in range(n_ctx)])

    def swap_chips(xs):
        return [xs[0]] + [
            lax.ppermute(xs[away], "ctx", [(i, i ^ (2 * away)) for i in range(n_ctx)]) for away in range(1, chips)
        ]

    got = swap_core(send)
    *pieces, rate_part = small_call(
        partial(merge_kernel, float(block), chips),
        "chip_stats",
        [group_doc, kept, got],
        [f32(6, part, LANES)] * chips + [f32(part, LANES)],
        [],
    )
    columns = pl.BlockSpec((1, block, SUBS, LANES), lambda i: (i, 0, 0, 0))
    z_local, w_local, zeros = pl.pallas_call(
        local_kernel,
        grid=(groups,),
        in_specs=[wide] * 4 + [slim, natural] + [chunked] * 2 + [pl.BlockSpec(memory_space=pl.ANY)],
        out_specs=[columns] * 2 + [pl.BlockSpec((1, LANES), lambda i: (0, 0))],
        out_shape=[pltpu.VMEM((groups, block, SUBS, LANES), F32)] * 2 + [pltpu.VMEM((1, LANES), F32)],
        scratch_shapes=[row_scratch] * 2 + [flat_scratch] + [mode_scratch] * 5 + [tap_scratch],
        compiler_params=params(BIG),
        cost_estimate=pl.CostEstimate(flops=10_000_000_000, bytes_accessed=20_000_000, transcendentals=0),
        name="local_outputs",
    )(k_in, v_in, q_in, g_in, vmem(rate), hbm(residue), vmem(ends), vmem(heads), rate_part)
    scanned = small_call(
        partial(scan_kernel, float(block), chips),
        "row_scan",
        [group_doc, rate_part, *swap_chips(pieces)],
        [f32(2, part, LANES)] * (chips + 1),
        [pltpu.VMEM((chips, 6, part, LANES), F32), pltpu.VMEM((chips, 2, part, LANES), F32)],
        after=[zeros],
    )
    total = scanned[chips]
    for other in [lax.ppermute(total, "dp", [(i, i ^ away) for i in range(n_dp)]) for away in range(1, n_dp)]:
        total = total + other
    held = [vmem(x) for x in (*tokens, rate, residue)]
    half_scratch = pltpu.VMEM((halves, SUBS, LANES), F32)
    in_vmem = pl.BlockSpec(memory_space=pltpu.VMEM)
    give, z_local, w_local = pl.pallas_call(
        partial(expand_kernel, float(block), chips),
        in_specs=[scalar_spec()] + [in_vmem] * (6 + chips),
        out_specs=[in_vmem] * 3,
        out_shape=[f32(2, half, LANES)] + [f32(groups, block, SUBS, LANES)] * 2,
        input_output_aliases={5: 1, 6: 2},
        scratch_shapes=[pltpu.VMEM((2, half, LANES), F32)] * 2
        + [pltpu.VMEM((GROUP // LANES * halves, LANES), F32)] + [half_scratch] * 3,
        compiler_params=params(),
        name="block_edges",
    )(group_doc, kept, got, rate, residue, z_local, w_local, *swap_chips(scanned[:chips]))
    theirs = swap_core(give).reshape(2, groups, halves, SUBS, LANES)

    def outputs(first, count, after, outs):
        wide, slim, natural, chunked, halved = specs(lambda i: i + first)
        columns = pl.BlockSpec((1, block, SUBS, LANES), lambda i: (i + first, 0, 0, 0))
        result = pl.pallas_call(
            partial(output_kernel, len(outs)),
            grid=(count,),
            in_specs=[wide] * 4 + [slim, natural] + [columns] * 2 + [halved(2)]
            + [pl.BlockSpec(memory_space=pl.ANY)] * (1 + len(outs)),
            out_specs=[wide] * 4 + [pl.BlockSpec((1, LANES), lambda i: (0, 0))],
            out_shape=[pltpu.HBM((block, channels), jnp.bfloat16)] * 4 + [pltpu.VMEM((1, LANES), F32)],
            input_output_aliases={10 + i: i for i in range(len(outs))},
            scratch_shapes=[row_scratch] * 2 + [flat_scratch] + [half_scratch] * 3,
            compiler_params=params(BIG),
            cost_estimate=pl.CostEstimate(
                flops=100_000_000 * count, bytes_accessed=500_000 * count, transcendentals=0
            ),
            name="outputs",
        )(*held, vmem(z_local), vmem(w_local), theirs, after, *outs)
        return result[:4], result[4]

    sums = swap_chips([total] * chips)
    cut = (3 * groups + 3) // 4
    outs, zeros = outputs(0, cut, total, [])
    (gathered,) = small_call(
        partial(gather_kernel, chips), "gather_sums", sums, [f32(2, half, LANES)], [], after=[zeros]
    )
    if cut < groups:
        outs, _ = outputs(cut, groups - cut, gathered, outs)
    residue_grad, pole_grad = small_call(
        partial(final_kernel, 1.0 / math.sqrt(total_tokens)),
        "parameter_grads",
        [rate, residue, gathered, swap_core(gathered)],
        [f32(modes, channels)] * 2,
        [pltpu.VMEM((2, rows, LANES), F32)] + [flat_scratch] * 2,
    )
    return (*(x[None] for x in outs), residue_grad, pole_grad)


def solution(mesh):
    tokens = P("dp", "ctx", None)
    return jax.shard_map(
        body,
        mesh=mesh,
        in_specs=(tokens, tokens, tokens, tokens, P(), P(), P("dp", None)),
        out_specs=(tokens, tokens, tokens, tokens, P(), P()),
        check_vma=False,
    )
```
